32 devices in a mesh: lon: 8 (over z, core), lat: 4 (over y, x).
Axes of the slice: x: 2, y: 2, z: 4, core: 2. Of those that a mesh axis runs over, the one named last changes fastest.
Arguments:
- tracers: float32 [2, 10, 256, 1024], P(None, None, 'lat', 'lon'), may hold values from -6 to 6
- velocity: float32 [2, 10, 256, 1024], P(None, None, 'lat', 'lon'), may hold values from -6 to 6
- active_levels: int32 [256, 1024], P('lat', 'lon'), may hold values from 0 to 10, as said below
- diffusivity: float32 [256, 1024], P('lat', 'lon'), may hold values from 0.02 to 0.2
- viscosity: float32 [256, 1024], P('lat', 'lon'), may hold values from 0.002 to 0.012
- ocean_depth: float32 [256, 1024], P('lat', 'lon'), may hold values from 0.5 to 1.5
- wind_forcing: float32 [2, 256, 1024], P(None, 'lat', 'lon'), may hold values from -5 to 5
Outputs:
- tracers_out: float32 [2, 10, 256, 1024], P(None, None, 'lat', 'lon')
- velocity_out: float32 [2, 10, 256, 1024], P(None, None, 'lat', 'lon')
- surface: float32 [256, 1024], P('lat', 'lon')
The draws below stay inside these ranges and needn't reach their ends.
Inputs may be any that keep to these rules, and one draw needn't show every extreme that they name: `active_levels`: 0 marks land, which covers whole aligned blocks of 8 x 8 cells; every other cell has 1 to 10 wet levels.
All inputs are finite; a program needn't handle non-finite values.
Results may differ from the reference program's by a relative error of at most 0.0003.
Values sent between devices are 32-bit elements; how exact they have to be, the bound alone decides.
A program may use at most 128 MiB of HBM per device.

```python
import math
import jax
import jax.numpy as jnp
from jax import lax

LEVELS = 10
SUBCYCLES = 8
SOLVE_ITERS = 4
NLAT = 256
NLON = 1024


def draw_active_levels(key, part):
    key = jax.random.fold_in(key, 11)
    land_key, level_key = jax.random.split(key)
    coarse = jax.random.randint(land_key, (NLAT // 8, NLON // 8), 0, 4)
    land_block = jnp.repeat(jnp.repeat(coarse == 0, 8, axis=0), 8, axis=1)
    levels = jax.random.randint(level_key, (NLAT, NLON), 1, LEVELS + 1)
    return jnp.where(land_block, 0, levels).astype(jnp.int32)


def block_levels(own_key, dims, cuts, low, largest):
    level = 1.0
    for dim, blocks in cuts:
        heights = jax.random.uniform(jax.random.fold_in(jax.random.fold_in(own_key, 6), dim), (blocks,), jnp.float32, low / len(cuts), largest / len(cuts))
        level = level * jnp.repeat(jnp.exp(heights), dims[dim] // blocks).reshape((-1,) + (1,) * (len(dims) - 1 - dim))
    return level


def normal_values(key, shape, width, bound, cuts=(), kind=jnp.bfloat16):
    factor_of = block_levels(key, shape, cuts, -0.22, 0.18) if cuts else 1.0
    entries = jax.random.normal(key, shape, jnp.float32) * width * factor_of
    return jnp.minimum(jnp.maximum(entries, -bound), bound).astype(kind)


def setup_inputs(seed: int = 0) -> dict:
    arg_keys = jax.random.split(jax.random.key(seed), 8)
    tracers = normal_values(arg_keys[0], (2, LEVELS, NLAT, NLON), 1.0, 6.0, ((2, 4), (3, 8)), jnp.float32)
    velocity = normal_values(arg_keys[1], (2, LEVELS, NLAT, NLON), 1.0, 6.0, ((2, 4), (3, 8)), jnp.float32)
    active_levels = draw_active_levels(jax.random.fold_in(arg_keys[7], 71), 0)
    diffusivity = jnp.clip(jnp.exp(math.log(0.2) - 2.3025851 * jax.random.uniform(arg_keys[3], (NLAT, NLON), jnp.float32) ** block_levels(arg_keys[3], (NLAT, NLON), ((0, 4), (1, 8)), -0.2, 0.2)), 0.02, 0.2)
    viscosity = jnp.clip(jnp.exp(math.log(0.012) - 1.7917594 * jax.random.uniform(arg_keys[4], (NLAT, NLON), jnp.float32) ** block_levels(arg_keys[4], (NLAT, NLON), ((0, 4), (1, 8)), -0.2, 0.2)), 0.002, 0.012)
    ocean_depth = jnp.clip(0.5 + 1.0 * jax.random.uniform(arg_keys[5], (NLAT, NLON), jnp.float32) ** block_levels(arg_keys[5], (NLAT, NLON), ((0, 4), (1, 8)), -0.2, 0.2), 0.5, 1.5)
    wind_forcing = normal_values(arg_keys[6], (2, NLAT, NLON), 1.0, 5.0, ((1, 4), (2, 8)), jnp.float32)
    return {"tracers": tracers, "velocity": velocity, "active_levels": active_levels, "diffusivity": diffusivity, "viscosity": viscosity, "ocean_depth": ocean_depth, "wind_forcing": wind_forcing}


edge_offsets = ((0, 1), (0, -1), (1, 0), (-1, 0))
corner_offsets = ((1, 1), (1, -1), (-1, 1), (-1, -1))
flow_step = 0.3
slope_step = 0.3
floor_diag = 0.05


def parity_of(values):
    return jnp.array(values, jnp.float32).reshape(-1, 1, 1)


def window(field, row_off, col_off):
    row_count = field.shape[-2] - 2
    col_count = field.shape[-1] - 2
    inner = lax.slice_in_dim(field, 1 + row_off, 1 + row_off + row_count, axis=field.ndim - 2)
    return lax.slice_in_dim(inner, 1 + col_off, 1 + col_off + col_count, axis=field.ndim - 1)


def masked_laplacian(field, coefficient, wet_mask):
    centre = window(field, 0, 0)
    mask_centre = window(wet_mask, 0, 0)
    summed = None
    for row_off, col_off in edge_offsets:
        face_weight = mask_centre * window(wet_mask, row_off, col_off)
        if coefficient is not None:
            face_weight = 0.5 * (window(coefficient, 0, 0) + window(coefficient, row_off, col_off)) * face_weight
        flux_term = face_weight * (window(field, row_off, col_off) - centre)
        summed = flux_term if summed is None else summed + flux_term
    return summed


def extend_global(stacked, margin, parity):
    lon_pad = jnp.concatenate([stacked[..., -margin:], stacked, stacked[..., :margin]], axis=-1)
    south_rows = jnp.zeros_like(lon_pad[:, :margin])
    north_rows = jnp.flip(lon_pad[:, -margin:], (1, 2)) * parity
    return jnp.concatenate([south_rows, lon_pad, north_rows], axis=1)


def nine_weights(statics):
    depth_pad = statics[0]
    ocean_pad = statics[1]
    depth_centre = window(depth_pad, 0, 0)
    ocean_centre = window(ocean_pad, 0, 0)
    weights = []
    for offsets, scale in ((edge_offsets, 1.0), (corner_offsets, 0.5)):
        for row_off, col_off in offsets:
            weights.append(scale * 0.5 * (depth_centre + window(depth_pad, row_off, col_off)) * ocean_centre * window(ocean_pad, row_off, col_off))
    diagonal = floor_diag * ocean_centre + (1.0 - ocean_centre)
    return weights, diagonal


def operate_nine(direction_pad, weights, diagonal):
    centre = window(direction_pad, 0, 0)
    summed = diagonal * centre
    for offset, weight in zip(edge_offsets + corner_offsets, weights):
        summed = summed + weight * (centre - window(direction_pad, offset[0], offset[1]))
    return summed


def barotropic(start_east, start_north, ocean_depth, ocean_mask):
    statics = extend_global(jnp.stack([ocean_depth, ocean_mask]), 1, parity_of([1.0, 1.0]))
    depth_pad = statics[0]
    height = jnp.zeros_like(start_east)
    east_flow, north_flow = start_east, start_north
    for cycle_index in range(SUBCYCLES):
        moved = extend_global(jnp.stack([east_flow, north_flow]), 1, parity_of([-1.0, -1.0]))
        flux_east = depth_pad * moved[0]
        flux_north = depth_pad * moved[1]
        divergence = 0.5 * ((window(flux_east, 0, 1) - window(flux_east, 0, -1)) + (window(flux_north, 1, 0) - window(flux_north, -1, 0)))
        height = height - flow_step * ocean_mask * divergence
        height_pad = extend_global(height[None], 1, parity_of([1.0]))[0]
        east_flow = east_flow - slope_step * ocean_mask * (0.5 * (window(height_pad, 0, 1) - window(height_pad, 0, -1)))
        north_flow = north_flow - slope_step * ocean_mask * (0.5 * (window(height_pad, 1, 0) - window(height_pad, -1, 0)))
    weights, diagonal = nine_weights(statics)
    surface = jnp.zeros_like(height)
    residual = height
    direction = height
    old_norm = jnp.sum(residual * residual)
    for iteration in range(SOLVE_ITERS):
        direction_pad = extend_global(direction[None], 1, parity_of([1.0]))[0]
        image = operate_nine(direction_pad, weights, diagonal)
        step_size = old_norm / jnp.sum(direction * image)
        surface = surface + step_size * direction
        residual = residual - step_size * image
        new_norm = jnp.sum(residual * residual)
        direction = residual + (new_norm / old_norm) * direction
        old_norm = new_norm
    surface_pad = extend_global(surface[None], 1, parity_of([1.0]))[0]
    east_final = east_flow - slope_step * ocean_mask * (0.5 * (window(surface_pad, 0, 1) - window(surface_pad, 0, -1)))
    north_final = north_flow - slope_step * ocean_mask * (0.5 * (window(surface_pad, 1, 0) - window(surface_pad, -1, 0)))
    return east_final, north_final, surface


def reference(tracers, velocity, active_levels, diffusivity, viscosity, ocean_depth, wind_forcing):
    levels_float = active_levels.astype(jnp.float32)
    statics = extend_global(jnp.stack([diffusivity, viscosity, levels_float]), 2, parity_of([1.0, 1.0, 1.0]))
    row_ids = jnp.arange(NLAT, dtype=jnp.float32)[:, None]
    coriolis = 0.25 * jnp.sin(math.pi * ((row_ids + 0.5) / NLAT - 0.5))

    def level_body(level, carry):
        tracer_store, star_store, column_sum = carry
        level_tracer = lax.dynamic_index_in_dim(tracers, level, 1, keepdims=False)
        level_velocity = lax.dynamic_index_in_dim(velocity, level, 1, keepdims=False)
        padded = extend_global(jnp.concatenate([level_tracer, level_velocity]), 2, parity_of([1.0, 1.0, -1.0, -1.0]))
        wet_pad = (level.astype(jnp.float32) < statics[2]).astype(jnp.float32)
        tracer_lap = window(masked_laplacian(padded[:2], statics[0], wet_pad), 0, 0)
        new_tracer = level_tracer + tracer_lap
        first_pass = masked_laplacian(padded[2:], None, wet_pad)
        second_pass = masked_laplacian(first_pass, window(statics[1], 0, 0), window(wet_pad, 0, 0))
        wet = wet_pad[2:-2, 2:-2]
        rotated = jnp.stack([level_velocity[1], -level_velocity[0]])
        star = wet * (level_velocity - second_pass + coriolis * rotated)
        tracer_store = lax.dynamic_update_index_in_dim(tracer_store, new_tracer, level, 1)
        star_store = lax.dynamic_update_index_in_dim(star_store, star, level, 1)
        return tracer_store, star_store, column_sum + star

    init = (jnp.zeros_like(tracers), jnp.zeros_like(velocity), jnp.zeros((2, NLAT, NLON), jnp.float32))
    tracers_out, star_all, column_sum = lax.fori_loop(0, LEVELS, level_body, init)
    column_mean = column_sum / jnp.maximum(levels_float, 1.0)
    ocean_mask = (active_levels > 0).astype(jnp.float32)
    start = column_mean + wind_forcing * ocean_mask
    east_final, north_final, surface = barotropic(start[0], start[1], ocean_depth, ocean_mask)
    corrected = jnp.stack([east_final, north_final])
    wet_all = (jnp.arange(LEVELS, dtype=jnp.float32)[:, None, None] < levels_float).astype(jnp.float32)
    velocity_out = star_all + wet_all * (corrected - column_mean)[:, None]
    return tracers_out, velocity_out, surface
```

```python
import functools
import math

import jax
import jax.numpy as jnp
from jax import lax
from jax.experimental import pallas as pl
from jax.experimental.pallas import tpu as pltpu
from jax.sharding import PartitionSpec as P

SUBCYCLES = 8
SOLVE_ITERS = 4
flow_step = 0.3
slope_step = 0.3
floor_diag = 0.05

PAD = 8
DEEP = 24
MESH = pl.DeviceIdType.MESH
F32 = jnp.float32

MID = floor_diag + 9.0
HALF = 9.0


def roll(x, shift, axis):
    return pltpu.roll(x, shift % x.shape[axis], axis)


def east(x):
    return roll(x, -1, x.ndim - 1)


def west(x):
    return roll(x, 1, x.ndim - 1)


def north(x):
    return roll(x, -1, x.ndim - 2)


def south(x):
    return roll(x, 1, x.ndim - 2)


def reversal(size):
    rows = lax.broadcasted_iota(jnp.int32, (size, size), 0)
    cols = lax.broadcasted_iota(jnp.int32, (size, size), 1)
    return jnp.where(rows + cols == size - 1, 1.0, 0.0).astype(F32)


def times(a, b):
    return jnp.dot(a, b, precision=lax.Precision.HIGHEST, preferred_element_type=F32)


def kernel(
    n_lon,
    n_lat,
    tracer_ref,
    velocity_ref,
    levels_ref,
    diff_ref,
    visc_ref,
    depth_ref,
    wind_ref,
    tracer_out,
    velocity_out,
    surface_out,
    fields,
    flats,
    firsts,
    near,
    statics,
    weights,
    flow,
    height,
    row_send,
    row_recv,
    col_send,
    col_recv,
    stat_recv,
    flow_recv,
    fold_recv,
    lat_sums,
    lon_sums,
    lat_parts,
    lon_parts,
    faces,
    send_sems,
    recv_sems,
    lat_send,
    lat_recv,
    lon_send,
    lon_recv,
):
    count = tracer_ref.shape[0] // 2
    rows, cols = levels_ref.shape
    top_row = PAD + rows
    lon = lax.axis_index("lon")
    lat = lax.axis_index("lat")
    right = lax.rem(lon + 1, n_lon)
    left = lax.rem(lon + n_lon - 1, n_lon)
    mirror = n_lon - 1 - lon
    top = lat == n_lat - 1
    bottom = lat == 0
    above = jnp.minimum(lat + 1, n_lat - 1)
    below = jnp.maximum(lat - 1, 0)

    def remote(src, dst, send, recv, device):
        return pltpu.make_async_remote_copy(
            src_ref=src, dst_ref=dst, send_sem=send, recv_sem=recv, device_id=device, device_id_type=MESH
        )

    barrier = pltpu.get_barrier_semaphore()
    for apart in range(1, n_lon):
        pl.semaphore_signal(
            barrier, inc=1, device_id={"lon": lax.rem(lon + apart, n_lon)}, device_id_type=MESH
        )
    for apart in range(1, n_lat):
        pl.semaphore_signal(
            barrier, inc=1, device_id={"lat": lax.rem(lat + apart, n_lat)}, device_id_type=MESH
        )

    kinds = 4 * count + 3
    packed = -(-2 * kinds // 8) * 8
    levels_float = levels_ref[...].astype(F32)
    flats[0, PAD:top_row, :] = visc_ref[...]
    flats[1, PAD:top_row, :] = diff_ref[...]
    flats[2, PAD:top_row, :] = levels_float
    fields[0 : 2 * count, PAD:top_row, :] = velocity_ref[...]
    fields[2 * count :, PAD:top_row, :] = tracer_ref[...]

    def block_of(k):
        return (fields, k) if k < 4 * count else (flats, k - 4 * count)

    for k in range(kinds):
        ref, index = block_of(k)
        row_send[0, 2 * k : 2 * k + 2, :] = ref[index, top_row - 2 : top_row, :]
        row_send[1, 2 * k : 2 * k + 1, :] = ref[index, PAD + 1 : PAD + 2, :]
        row_send[1, 2 * k + 1 : 2 * k + 2, :] = ref[index, PAD : PAD + 1, :]
    row_send[:, 2 * kinds : packed, :] = jnp.zeros((2, packed - 2 * kinds, cols), F32)
    statics[0, DEEP : DEEP + rows, 0:cols] = depth_ref[...]
    statics[1, DEEP : DEEP + rows, 0:cols] = levels_float
    for f in range(2):
        at = packed + f * DEEP
        row_send[0, at : at + DEEP, :] = statics[f, rows : rows + DEEP, 0:cols]
        row_send[1, at : at + DEEP, :] = statics[f, DEEP : 2 * DEEP, 0:cols]

    pl.semaphore_wait(barrier, n_lon + n_lat - 2)

    def rows_out(src, dst, stage):
        @pl.when(top)
        def _():
            remote(src(0), dst(0), send_sems.at[stage, 0], recv_sems.at[stage, 0], {"lon": mirror}).start()

        @pl.when(jnp.logical_not(top))
        def _():
            remote(src(0), dst(1), send_sems.at[stage, 0], recv_sems.at[stage, 1], {"lat": above}).start()

        @pl.when(jnp.logical_not(bottom))
        def _():
            remote(src(1), dst(0), send_sems.at[stage, 1], recv_sems.at[stage, 0], {"lat": below}).start()

    def rows_in(src, dst, stage):
        remote(src(0), dst(0), send_sems.at[stage, 0], recv_sems.at[stage, 0], {"lat": above}).wait_recv()

        @pl.when(jnp.logical_not(bottom))
        def _():
            remote(src(1), dst(1), send_sems.at[stage, 1], recv_sems.at[stage, 1], {"lat": below}).wait_recv()

    def rows_sent(src, dst, stage):
        remote(src(0), dst(0), send_sems.at[stage, 0], recv_sems.at[stage, 0], {"lat": above}).wait_send()

        @pl.when(jnp.logical_not(bottom))
        def _():
            remote(src(1), dst(1), send_sems.at[stage, 1], recv_sems.at[stage, 1], {"lat": below}).wait_send()

    def cols_copies(to_east, to_west, dst, stage):
        return (
            remote(to_east, dst(0), send_sems.at[stage, 0], recv_sems.at[stage, 0], {"lon": right}),
            remote(to_west, dst(1), send_sems.at[stage, 1], recv_sems.at[stage, 1], {"lon": left}),
        )

    row_src = lambda i: row_send.at[i]
    row_dst = lambda i: row_recv.at[i]

    @pl.when(bottom)
    def _():
        row_recv[1] = jnp.zeros(row_recv.shape[1:], F32)

    rows_out(row_src, row_dst, 0)

    lane = lax.broadcasted_iota(jnp.int32, (rows, cols), 1)
    own = jnp.zeros((rows, cols), F32)
    inner = jnp.zeros((rows, cols), F32)
    for k in range(kinds):
        ref, index = block_of(k)
        x = ref[index, PAD:top_row, :]
        pair = jnp.right_shift(lane, 1) == k
        own = jnp.where(pair, roll(x, 2 * k + 1, 1), own)
        if k < 2 * count or k == kinds - 1:
            odd_part = jnp.bitwise_and(lane, 1) == 1
            inner = jnp.where(pair, jnp.where(odd_part, roll(x, 2 * k, 1), roll(x, 2 * k + 2, 1)), inner)

    rows_in(row_src, row_dst, 0)

    @pl.when(top)
    def _():
        back = reversal(cols)
        turned = times(row_recv[0], back)
        ids = lax.broadcasted_iota(jnp.int32, turned.shape, 0)
        row_recv[0] = jnp.where(ids < 4 * count, -turned, turned)
        for f in range(2):
            at = packed + f * DEEP
            row_recv[0, at : at + DEEP, :] = times(reversal(DEEP), row_recv[0, at : at + DEEP, :])

    for k in range(kinds):
        ref, index = block_of(k)
        ref[index, top_row : top_row + 1, :] = row_recv[0, 2 * k + 1 : 2 * k + 2, :]
        ref[index, top_row + 1 : top_row + 2, :] = row_recv[0, 2 * k : 2 * k + 1, :]
        ref[index, PAD - 2 : PAD, :] = row_recv[1, 2 * k : 2 * k + 2, :]
    for f in range(2):
        at = packed + f * DEEP
        statics[f, 0:DEEP, 0:cols] = row_recv[1, at : at + DEEP, :]
        statics[f, DEEP + rows :, 0:cols] = row_recv[0, at : at + DEEP, :]

    tall = rows + 2 * PAD
    lane = lax.broadcasted_iota(jnp.int32, (tall, cols), 1)
    odd = jnp.bitwise_and(lane, 1) == 1

    def corner(received):
        square = jnp.concatenate([received, jnp.zeros((cols - packed, cols), F32)], axis=0)
        turned = jnp.transpose(square)
        lane_row = lax.broadcasted_iota(jnp.int32, (1, cols), 1)
        return jnp.where(
            jnp.bitwise_and(lane_row, 1) == 1,
            turned[0:1, :],
            roll(turned[cols - PAD :, :], -1, 1)[PAD - 1 :, :],
        )

    near[0] = jnp.zeros((tall, cols), F32)
    near[1] = jnp.zeros((tall, cols), F32)
    near[0, PAD:top_row, :] = own
    near[1, PAD:top_row, :] = inner
    near[0, PAD - 1 : PAD, :] = corner(row_recv[1, 0:packed, :])
    near[0, top_row : top_row + 1, :] = corner(row_recv[0, 0:packed, :])
    own, inner = near[0], near[1]
    col_send[1] = jnp.where(odd, own, east(inner))
    col_send[0] = jnp.where(odd, west(inner), own)
    col_send[1] = jnp.where(odd, own, roll(inner, -1, 1))
    col_send[0] = jnp.where(odd, roll(inner, 1, 1), own)
    cols_dst = lambda i: col_recv.at[i]
    stat_dst = lambda i: stat_recv.at[i]
    stat_src = statics.at[:, :, 0:cols]
    col_copies = cols_copies(col_send.at[0], col_send.at[1], cols_dst, 1)
    stat_copies = cols_copies(stat_src, stat_src, stat_dst, 2)
    for copy in col_copies + stat_copies:
        copy.start()
    rows_sent(row_src, row_dst, 0)
    for copy in col_copies:
        copy.wait_recv()

    from_west, from_east = col_recv[0], col_recv[1]
    close = jnp.where(odd, roll(from_west, 1, 1), roll(from_east, -1, 1))
    far = jnp.where(odd, from_west, from_east)
    near[1] = close

    field_of = jnp.right_shift(lane, 1)
    level_of = lax.rem(field_of, count).astype(F32)

    def packed_wet(pack):
        at = 2 * (kinds - 1)
        level = jnp.where(odd, pack[:, at + 1 : at + 2], pack[:, at : at + 1])
        return jnp.where(level_of < level, 1.0, 0.0)

    wet_own, wet_close, wet_far = packed_wet(own), packed_wet(close), packed_wet(far)
    firsts[...] = wet_close * (
        wet_own * (own - close)
        + wet_far * (far - close)
        + north(wet_close) * (north(close) - close)
        + south(wet_close) * (south(close) - close)
    )

    first_lane, last_lane = lane == 0, lane == cols - 1

    def sides(x, pack, k):
        rim = pltpu.roll(pack, cols - 1 - 2 * k, 1)
        return jnp.where(last_lane, rim, east(x)), jnp.where(first_lane, rim, west(x))

    for index in range(2):
        c = flats[index]
        c_east, c_west = sides(c, close, 4 * count + index)
        for n, other in enumerate((c_east, c_west, north(c), south(c))):
            faces[index, n] = 0.5 * (c + other)
    depth_levels = flats[2]
    lev_east, lev_west = sides(depth_levels, close, kinds - 1)
    faces[2, 0] = lev_east
    faces[2, 1] = lev_west

    row_ids = (lat * rows + lax.broadcasted_iota(jnp.int32, (rows, cols), 0)).astype(F32)
    coriolis = 0.25 * jnp.sin(math.pi * ((row_ids + 0.5) / (rows * n_lat) - 0.5))

    def wet_sides(level):
        wet = jnp.where(level < flats[2], 1.0, 0.0)
        return (
            wet,
            wet * jnp.where(level < faces[2, 0], 1.0, 0.0),
            wet * jnp.where(level < faces[2, 1], 1.0, 0.0),
            wet * north(wet),
            wet * south(wet),
        )

    surface_out[...] = jnp.zeros((rows, cols), F32)
    flow[...] = jnp.zeros(flow.shape, F32)

    def velocity_level(level, carry):
        wet, w_east, w_west, w_north, w_south = wet_sides(level.astype(F32))
        coefficient = [faces[0, n] * w for n, w in enumerate((w_east, w_west, w_north, w_south))]
        wet_centre = wet[PAD:top_row]
        pair = []
        for comp in range(2):
            k = comp * count + level
            x = fields[k]
            x_east, x_west = sides(x, near[1], k)
            first = (
                w_east * (x_east - x)
                + w_west * (x_west - x)
                + w_north * (north(x) - x)
                + w_south * (south(x) - x)
            )
            f_east, f_west = sides(first, firsts[...], k)
            second = (
                coefficient[0] * (f_east - first)
                + coefficient[1] * (f_west - first)
                + coefficient[2] * (north(first) - first)
                + coefficient[3] * (south(first) - first)
            )
            pair.append((x[PAD:top_row], second[PAD:top_row]))
        (u, lap_u), (v, lap_v) = pair
        star_u = wet_centre * (u - lap_u + coriolis * v)
        star_v = wet_centre * (v - lap_v - coriolis * u)
        velocity_out[level] = star_u
        velocity_out[count + level] = star_v
        flow[0, DEEP : DEEP + rows, 0:cols] += star_u
        flow[1, DEEP : DEEP + rows, 0:cols] += star_v
        return carry

    lax.fori_loop(0, count, velocity_level, 0)

    levels_here = flats[2, PAD:top_row, :]
    ocean_here = jnp.where(levels_here > 0, 1.0, 0.0)
    for comp in range(2):
        mean = flow[comp, DEEP : DEEP + rows, 0:cols] / jnp.maximum(levels_here, 1.0)
        height[1 + comp, 0:rows, 0:cols] = mean
        flow[comp, DEEP : DEEP + rows, 0:cols] = mean + wind_ref[comp] * ocean_here

    flow_edge = lambda i: flow.at[:, rows : rows + DEEP, 0:cols] if i == 0 else flow.at[:, DEEP : 2 * DEEP, 0:cols]
    fold_dst = lambda i: fold_recv.at[i]
    rows_out(flow_edge, fold_dst, 3)

    def tracer_level(level, carry):
        _, w_east, w_west, w_north, w_south = wet_sides(level.astype(F32))
        coefficient = [faces[1, n] * w for n, w in enumerate((w_east, w_west, w_north, w_south))]
        for comp in range(2):
            k = comp * count + level
            x = fields[2 * count + k]
            x_east, x_west = sides(x, near[1], 2 * count + k)
            change = (
                coefficient[0] * (x_east - x)
                + coefficient[1] * (x_west - x)
                + coefficient[2] * (north(x) - x)
                + coefficient[3] * (south(x) - x)
            )
            tracer_out[k] = (x + change)[PAD:top_row]
        return carry

    lax.fori_loop(0, count // 2, tracer_level, 0)

    rows_in(flow_edge, fold_dst, 3)

    @pl.when(top)
    def _():
        for comp in range(2):
            turned = times(fold_recv[0, comp], reversal(cols))
            fold_recv[0, comp] = -times(reversal(DEEP), turned)

    for comp in range(2):
        flow[comp, DEEP + rows :, 0:cols] = fold_recv[0, comp]

    @pl.when(jnp.logical_not(bottom))
    def _():
        for comp in range(2):
            flow[comp, 0:DEEP, 0:cols] = fold_recv[1, comp]

    flow_src = flow.at[:, :, 0:cols]
    flow_dst = lambda i: flow_recv.at[i]
    flow_copies = cols_copies(flow_src, flow_src, flow_dst, 4)
    for copy in flow_copies:
        copy.start()
    lax.fori_loop(count // 2, count, tracer_level, 0)
    rows_sent(flow_edge, fold_dst, 3)

    for copy in stat_copies:
        copy.wait_recv()
    deep_rows = rows + 2 * DEEP
    half = lax.broadcasted_iota(jnp.int32, (deep_rows, cols), 1) < cols // 2
    for f in range(2):
        statics[f, :, cols:] = jnp.where(half, stat_recv[1, f], stat_recv[0, f])
    depth = statics[0]
    ocean = jnp.where(statics[1] > 0, 1.0, 0.0)
    ocean_ref = weights.at[9]
    ocean_ref[...] = ocean
    total = floor_diag * ocean + (1.0 - ocean)
    shifts = []
    for move in (lambda x: x, north, south):
        d, o = move(depth), move(ocean)
        if move in (north, south):
            shifts.append((1.0, d, o))
        scale = 0.5 if move in (north, south) else 1.0
        shifts.append((scale, east(d), east(o)))
        shifts.append((scale, west(d), west(o)))
    for n, (scale, d, o) in enumerate(shifts):
        weight = scale * 0.5 * (depth + d) * ocean * o
        weights[n] = weight
        total = total + weight
    weights[8] = total

    for copy in flow_copies:
        copy.wait_recv()
    for copy in flow_copies:
        copy.wait_send()
    for comp in range(2):
        flow[comp, :, cols:] = jnp.where(half, flow_recv[1, comp], flow_recv[0, comp])

    height[0] = jnp.zeros(height.shape[1:], F32)

    def subcycle(step, carry):
        flux_east = statics[0] * flow[0]
        flux_north = statics[0] * flow[1]
        ocean_now = weights[9]
        divergence = (east(flux_east) - west(flux_east)) + (north(flux_north) - south(flux_north))
        high = height[0] - (0.5 * flow_step) * ocean_now * divergence
        height[0] = high
        flow[0] = flow[0] - (0.5 * slope_step) * ocean_now * (east(high) - west(high))
        flow[1] = flow[1] - (0.5 * slope_step) * ocean_now * (north(high) - south(high))
        return carry

    lax.fori_loop(0, SUBCYCLES, subcycle, 0)

    def operate(p):
        up, down = north(p), south(p)
        summed = weights[8] * p - weights[0] * east(p) - weights[1] * west(p)
        summed = summed - weights[2] * up - weights[3] * east(up) - weights[4] * west(up)
        return summed - weights[5] * down - weights[6] * east(down) - weights[7] * west(down)

    basis = [height[0]]
    for n in range(SOLVE_ITERS):
        v = basis[-1]
        scaled = (operate(v) - MID * v) * ((1.0 if n == 0 else 2.0) / HALF)
        basis.append(scaled if n == 0 else scaled - basis[-2])

    pairs = [(i, j) for i in range(SOLVE_ITERS) for j in range(i, SOLVE_ITERS + 1)]
    inside = [v[DEEP : DEEP + rows, 0:cols] for v in basis]
    lat_parts[...] = jnp.zeros(lat_parts.shape, F32)
    for n, (i, j) in enumerate(pairs):
        lat_parts[n : n + 1, :] = jnp.sum(inside[i] * inside[j], axis=0, keepdims=True)

    def all_sum(parts, slots, sends, recvs, axis, me, size):
        copies = [
            remote(parts, slots.at[d - 1], sends.at[d - 1], recvs.at[d - 1], {axis: lax.rem(me + d, size)})
            for d in range(1, size)
        ]
        for copy in copies:
            copy.start()
        for copy in copies:
            copy.wait()
        result = parts[...]
        for d in range(1, size):
            result = result + slots[d - 1]
        return result

    lon_parts[...] = all_sum(lat_parts, lat_sums, lat_send, lat_recv, "lat", lat, n_lat)
    sums = jnp.sum(
        all_sum(lon_parts, lon_sums, lon_send, lon_recv, "lon", lon, n_lon), axis=1, keepdims=True
    )
    gram = {}
    for n, (i, j) in enumerate(pairs):
        gram[i, j] = gram[j, i] = sums[n : n + 1, :]

    def inner_product(a, b):
        result = None
        for i, x in a.items():
            for j, y in b.items():
                term = x * y * gram[i, j]
                result = term if result is None else result + term
        return result

    def image_of(a):
        result = {}

        def add(n, value):
            result[n] = result[n] + value if n in result else value

        for n, x in a.items():
            add(n, MID * x)
            add(n + 1, (HALF if n == 0 else 0.5 * HALF) * x)
            if n > 0:
                add(n - 1, 0.5 * HALF * x)
        return result

    one = jnp.ones((1, 1), F32)
    residual = {0: one}
    direction = {0: one}
    answer = {}
    norm = inner_product(residual, residual)
    for iteration in range(SOLVE_ITERS):
        image = image_of(direction)
        step = norm / inner_product(direction, image)
        for n, x in direction.items():
            answer[n] = answer[n] + step * x if n in answer else step * x
        if iteration < SOLVE_ITERS - 1:
            residual = {n: (residual[n] if n in residual else 0.0) - step * x for n, x in image.items()}
            new_norm = inner_product(residual, residual)
            ratio = new_norm / norm
            direction = {
                n: x + ratio * direction[n] if n in direction else x for n, x in residual.items()
            }
            norm = new_norm
    surface = None
    for n, x in answer.items():
        term = x * basis[n]
        surface = term if surface is None else surface + term
    surface_out[...] = surface[DEEP : DEEP + rows, 0:cols]

    slopes = (east(surface) - west(surface), north(surface) - south(surface))
    for comp, slope in enumerate(slopes):
        final = flow[comp] - (0.5 * slope_step) * weights[9] * slope
        height[1 + comp, 0:rows, 0:cols] = final[DEEP : DEEP + rows, 0:cols] - height[1 + comp, 0:rows, 0:cols]

    def correct(level, carry):
        wet = level.astype(F32) < flats[2, PAD:top_row, :]
        for comp in range(2):
            k = comp * count + level
            velocity_out[k] = velocity_out[k] + jnp.where(wet, height[1 + comp, 0:rows, 0:cols], 0.0)
        return carry

    lax.fori_loop(0, count, correct, 0)
    for copy in col_copies + stat_copies:
        copy.wait_send()


def per_device(n_lon, n_lat, tracers, velocity, active_levels, diffusivity, viscosity, ocean_depth, wind_forcing):
    _, count, rows, cols = tracers.shape
    kinds = 4 * count + 3
    packed = -(-2 * kinds // 8) * 8
    message = packed + 2 * DEEP
    tall, deep_rows = rows + 2 * PAD, rows + 2 * DEEP
    entries = 16
    block = jax.ShapeDtypeStruct((2 * count, rows, cols), F32)
    vmem = pl.BlockSpec(memory_space=pltpu.VMEM)
    out = pl.pallas_call(
        functools.partial(kernel, n_lon, n_lat),
        out_shape=(block, block, jax.ShapeDtypeStruct((rows, cols), F32)),
        in_specs=[vmem] * 7,
        out_specs=(vmem, vmem, vmem),
        scratch_shapes=[
            pltpu.VMEM((4 * count, tall, cols), F32),
            pltpu.VMEM((3, tall, cols), F32),
            pltpu.VMEM((tall, cols), F32),
            pltpu.VMEM((2, tall, cols), F32),
            pltpu.VMEM((2, deep_rows, 2 * cols), F32),
            pltpu.VMEM((10, deep_rows, 2 * cols), F32),
            pltpu.VMEM((2, deep_rows, 2 * cols), F32),
            pltpu.VMEM((3, deep_rows, 2 * cols), F32),
            pltpu.VMEM((2, message, cols), F32),
            pltpu.VMEM((2, message, cols), F32),
            pltpu.VMEM((2, tall, cols), F32),
            pltpu.VMEM((2, tall, cols), F32),
            pltpu.VMEM((2, 2, deep_rows, cols), F32),
            pltpu.VMEM((2, 2, deep_rows, cols), F32),
            pltpu.VMEM((2, 2, DEEP, cols), F32),
            pltpu.VMEM((n_lat - 1, entries, cols), F32),
            pltpu.VMEM((n_lon - 1, entries, cols), F32),
            pltpu.VMEM((entries, cols), F32),
            pltpu.VMEM((entries, cols), F32),
            pltpu.VMEM((3, 4, tall, cols), F32),
            pltpu.SemaphoreType.DMA((5, 2)),
            pltpu.SemaphoreType.DMA((5, 2)),
            pltpu.SemaphoreType.DMA((n_lat - 1,)),
            pltpu.SemaphoreType.DMA((n_lat - 1,)),
            pltpu.SemaphoreType.DMA((n_lon - 1,)),
            pltpu.SemaphoreType.DMA((n_lon - 1,)),
        ],
        compiler_params=pltpu.CompilerParams(
            collective_id=0, has_side_effects=True, vmem_limit_bytes=40 * 1024 * 1024
        ),
    )(
        tracers.reshape(2 * count, rows, cols),
        velocity.reshape(2 * count, rows, cols),
        active_levels,
        diffusivity,
        viscosity,
        ocean_depth,
        wind_forcing,
    )
    return out[0].reshape(tracers.shape), out[1].reshape(velocity.shape), out[2]


def solution(mesh):
    flat = P("lat", "lon")
    deep = P(None, None, "lat", "lon")
    return jax.shard_map(
        functools.partial(per_device, mesh.shape["lon"], mesh.shape["lat"]),
        mesh=mesh,
        in_specs=(deep, deep, flat, flat, flat, flat, P(None, "lat", "lon")),
        out_specs=(deep, deep, flat),
        check_vma=False,
    )
```

```python
import functools
import math

import jax
import jax.numpy as jnp
from jax import lax
from jax.experimental import pallas as pl
from jax.experimental.pallas import tpu as pltpu
from jax.sharding import PartitionSpec as P

SUBCYCLES = 8
SOLVE_ITERS = 4
flow_step = 0.3
slope_step = 0.3
floor_diag = 0.05

PAD = 8
DEEP = 24
STRIP = 32
MESH = pl.DeviceIdType.MESH
F32 = jnp.float32

SHIFTS = (0.0, 5.0, 2.5, 8.0)
SCALE = 5.0


def roll(x, shift, axis):
    return pltpu.roll(x, shift % x.shape[axis], axis)


def lanes(shape):
    return lax.broadcasted_iota(jnp.int32, shape, len(shape) - 1)


def lane_sides(a, b):
    cols = a.shape[-1]
    lane = lanes(a.shape)
    last, first = lane == cols - 1, lane == 0
    a_up, b_up = roll(a, -1, 1), roll(b, -1, 1)
    a_down, b_down = roll(a, 1, 1), roll(b, 1, 1)
    east = (jnp.where(last, b_up, a_up), jnp.where(last, a_up, b_up))
    west = (jnp.where(first, b_down, a_down), jnp.where(first, a_down, b_down))
    return east, west


def mirrored(x):
    return jnp.take_along_axis(x, x.shape[1] - 1 - lanes(x.shape), axis=1)


def kernel(
    n_lon,
    n_lat,
    tracer_hbm,
    velocity_hbm,
    levels_hbm,
    diff_hbm,
    visc_hbm,
    depth_hbm,
    wind_hbm,
    tracer_out,
    star_out,
    extra_out,
    fields,
    flats,
    levels_in,
    wind,
    near,
    firsts,
    laps,
    faces,
    deep,
    ocean,
    weights,
    flux,
    basis,
    row_send,
    row_recv,
    col_send,
    col_recv,
    strip_send,
    strip_recv,
    fold_recv,
    lat_sums,
    lon_sums,
    lat_parts,
    lon_parts,
    load_sems,
    send_sems,
    recv_sems,
    lat_send,
    lat_recv,
    lon_send,
    lon_recv,
):
    count = tracer_hbm.shape[0] // 2
    rows, cols = levels_hbm.shape
    top_row = PAD + rows
    deep_rows = rows + 2 * DEEP
    start = PAD + DEEP
    stop = start + rows
    end = PAD + deep_rows
    lon = lax.axis_index("lon")
    lat = lax.axis_index("lat")
    right = lax.rem(lon + 1, n_lon)
    left = lax.rem(lon + n_lon - 1, n_lon)
    mirror = n_lon - 1 - lon
    top = lat == n_lat - 1
    bottom = lat == 0
    above = jnp.minimum(lat + 1, n_lat - 1)
    below = jnp.maximum(lat - 1, 0)

    loads = [
        pltpu.make_async_copy(src, dst, load_sems.at[n])
        for n, (src, dst) in enumerate(
            (
                (velocity_hbm, fields.at[0 : 2 * count, PAD:top_row, :]),
                (tracer_hbm, fields.at[2 * count : 4 * count, PAD:top_row, :]),
                (levels_hbm, levels_in),
                (visc_hbm, flats.at[0, PAD:top_row, :]),
                (diff_hbm, flats.at[1, PAD:top_row, :]),
                (depth_hbm, deep.at[0, 0, start:stop, :]),
                (wind_hbm, wind),
            )
        )
    ]
    for load in loads:
        load.start()

    def remote(src, dst, send, recv, device):
        return pltpu.make_async_remote_copy(
            src_ref=src, dst_ref=dst, send_sem=send, recv_sem=recv, device_id=device, device_id_type=MESH
        )

    barrier = pltpu.get_barrier_semaphore()
    for apart in range(1, n_lon):
        pl.semaphore_signal(
            barrier, inc=1, device_id={"lon": lax.rem(lon + apart, n_lon)}, device_id_type=MESH
        )
    for apart in range(1, n_lat):
        pl.semaphore_signal(
            barrier, inc=1, device_id={"lat": lax.rem(lat + apart, n_lat)}, device_id_type=MESH
        )

    kinds = 4 * count + 3
    packed = -(-2 * kinds // 8) * 8
    row_send[:, 2 * kinds : packed, :] = jnp.zeros((2, packed - 2 * kinds, cols), F32)
    deep[2:4] = jnp.zeros((2,) + deep.shape[1:], F32)
    for array in (flux, ocean):
        array[:, 0:PAD, :] = jnp.zeros((2, PAD, cols), F32)
        array[:, end:, :] = jnp.zeros((2, PAD, cols), F32)
    for array in (basis, deep.at[0:2]):
        array[:, :, 0:PAD, :] = jnp.zeros((array.shape[0], 2, PAD, cols), F32)
        array[:, :, end:, :] = jnp.zeros((array.shape[0], 2, PAD, cols), F32)
    basis[0, :, PAD:end, :] = jnp.zeros((2, deep_rows, cols), F32)
    laps[...] = jnp.zeros(laps.shape, F32)
    for n in range(2):
        near[n] = jnp.zeros(near.shape[1:], F32)

    @pl.when(bottom)
    def _():
        row_recv[1] = jnp.zeros(row_recv.shape[1:], F32)

    for load in loads:
        load.wait()

    levels_float = levels_in[...].astype(F32)
    flats[2, PAD:top_row, :] = levels_float
    deep[1, 0, start:stop, :] = levels_float

    def block_of(k):
        return (fields, k) if k < 4 * count else (flats, k - 4 * count)

    for k in range(kinds):
        ref, index = block_of(k)
        row_send[0, 2 * k : 2 * k + 2, :] = ref[index, top_row - 2 : top_row, :]
        row_send[1, 2 * k : 2 * k + 1, :] = ref[index, PAD + 1 : PAD + 2, :]
        row_send[1, 2 * k + 1 : 2 * k + 2, :] = ref[index, PAD : PAD + 1, :]
    for f in range(2):
        at = packed + f * DEEP
        row_send[0, at : at + DEEP, :] = deep[f, 0, stop - DEEP : stop, :]
        row_send[1, at : at + DEEP, :] = deep[f, 0, start : start + DEEP, :]

    pl.semaphore_wait(barrier, n_lon + n_lat - 2)

    def rows_out(src, dst, stage):
        @pl.when(top)
        def _():
            remote(src(0), dst(0), send_sems.at[stage, 0], recv_sems.at[stage, 0], {"lon": mirror}).start()

        @pl.when(jnp.logical_not(top))
        def _():
            remote(src(0), dst(1), send_sems.at[stage, 0], recv_sems.at[stage, 1], {"lat": above}).start()

        @pl.when(jnp.logical_not(bottom))
        def _():
            remote(src(1), dst(0), send_sems.at[stage, 1], recv_sems.at[stage, 0], {"lat": below}).start()

    def rows_in(src, dst, stage):
        remote(src(0), dst(0), send_sems.at[stage, 0], recv_sems.at[stage, 0], {"lat": above}).wait_recv()

        @pl.when(jnp.logical_not(bottom))
        def _():
            remote(src(1), dst(1), send_sems.at[stage, 1], recv_sems.at[stage, 1], {"lat": below}).wait_recv()

    def rows_sent(src, dst, stage):
        remote(src(0), dst(0), send_sems.at[stage, 0], recv_sems.at[stage, 0], {"lat": above}).wait_send()

        @pl.when(jnp.logical_not(bottom))
        def _():
            remote(src(1), dst(1), send_sems.at[stage, 1], recv_sems.at[stage, 1], {"lat": below}).wait_send()

    def cols_copies(send, recv, stage):
        return (
            remote(send.at[0], recv.at[0], send_sems.at[stage, 0], recv_sems.at[stage, 0], {"lon": right}),
            remote(send.at[1], recv.at[1], send_sems.at[stage, 1], recv_sems.at[stage, 1], {"lon": left}),
        )

    row_src = lambda i: row_send.at[i]
    row_dst = lambda i: row_recv.at[i]
    rows_out(row_src, row_dst, 0)

    lane = lanes((rows, cols))
    own = jnp.zeros((rows, cols), F32)
    inner = jnp.zeros((rows, cols), F32)
    odd_here = jnp.bitwise_and(lane, 1) == 1
    for k in range(kinds):
        ref, index = block_of(k)
        x = ref[index, PAD:top_row, :]
        pair = jnp.right_shift(lane, 1) == k
        own = jnp.where(pair, roll(x, 2 * k + 1, 1), own)
        if k < 2 * count or k == kinds - 1:
            inner = jnp.where(pair, jnp.where(odd_here, roll(x, 2 * k, 1), roll(x, 2 * k + 2, 1)), inner)
    near[0, PAD:top_row, :] = own
    near[1, PAD:top_row, :] = inner

    rows_in(row_src, row_dst, 0)

    @pl.when(top)
    def _():
        turned = mirrored(row_recv[0])
        ids = lax.broadcasted_iota(jnp.int32, turned.shape, 0)
        turned = jnp.where(ids < 4 * count, -turned, turned)
        row_recv[0, 0:packed, :] = turned[0:packed]
        for f in range(2):
            at = packed + f * DEEP
            for n in range(DEEP):
                row_recv[0, at + n : at + n + 1, :] = turned[at + DEEP - 1 - n : at + DEEP - n]

    for f in range(2):
        at = packed + f * DEEP
        deep[f, 0, PAD:start, :] = row_recv[1, at : at + DEEP, :]
        deep[f, 0, stop:end, :] = row_recv[0, at : at + DEEP, :]

    tall = rows + 2 * PAD
    lane = lanes((tall, cols))
    odd = jnp.bitwise_and(lane, 1) == 1

    def corner(received):
        square = jnp.concatenate([received, jnp.zeros((cols - packed, cols), F32)], axis=0)
        turned = jnp.transpose(square)
        return jnp.where(
            jnp.bitwise_and(lanes((1, cols)), 1) == 1,
            turned[0:1, :],
            roll(turned[cols - PAD :, :], -1, 1)[PAD - 1 :, :],
        )

    near[0, PAD - 1 : PAD, :] = corner(row_recv[1, 0:packed, :])
    near[0, top_row : top_row + 1, :] = corner(row_recv[0, 0:packed, :])
    own, inner = near[0], near[1]
    col_send[1] = jnp.where(odd, own, roll(inner, -1, 1))
    col_send[0] = jnp.where(odd, roll(inner, 1, 1), own)
    col_copies = cols_copies(col_send, col_recv, 1)
    for copy in col_copies:
        copy.start()

    groups = cols // STRIP
    tiles = deep_rows // 8
    group_of = lanes((8, cols)) // STRIP

    def pack_strips(pair, f):
        for side, base in ((0, cols - STRIP), (1, 0)):
            for t in range(0, tiles, groups):
                strip = None
                for g in range(min(groups, tiles - t)):
                    at = PAD + 8 * (t + g)
                    x = roll(deep[2 * pair + f, 0, at : at + 8, :], STRIP * g - base, 1)
                    strip = x if strip is None else jnp.where(group_of == g, x, strip)
                strip_send[pair, side, f, 8 * (t // groups) : 8 * (t // groups) + 8, :] = strip

    def unpack_strips(pair, f):
        for j in range(tiles):
            at, t, g = PAD + 8 * j, 8 * (j // groups), j % groups
            low = roll(strip_recv[pair, 1, f, t : t + 8, :], -STRIP * g, 1)
            high = roll(strip_recv[pair, 0, f, t : t + 8, :], cols - STRIP - STRIP * g, 1)
            deep[2 * pair + f, 1, at : at + 8, :] = jnp.where(group_of < groups // 2, low, high)

    for f in range(2):
        pack_strips(0, f)
    stat_copies = cols_copies(strip_send.at[0], strip_recv.at[0], 2)
    for copy in stat_copies:
        copy.start()

    for k in range(kinds):
        ref, index = block_of(k)
        ref[index, top_row : top_row + 1, :] = row_recv[0, 2 * k + 1 : 2 * k + 2, :]
        ref[index, top_row + 1 : top_row + 2, :] = row_recv[0, 2 * k : 2 * k + 1, :]
        ref[index, PAD - 2 : PAD, :] = row_recv[1, 2 * k : 2 * k + 2, :]

    row_ids = (lat * rows + lax.broadcasted_iota(jnp.int32, (rows, cols), 0)).astype(F32)
    coriolis = 0.25 * jnp.sin(math.pi * ((row_ids + 0.5) / (rows * n_lat) - 0.5))
    faces[2, 2, 0:rows, :] = coriolis

    for copy in col_copies:
        copy.wait_recv()
    from_west, from_east = col_recv[0], col_recv[1]
    close = jnp.where(odd, roll(from_west, 1, 1), roll(from_east, -1, 1))
    far = jnp.where(odd, from_west, from_east)
    near[1] = close

    level_of = lax.rem(jnp.right_shift(lane, 1), count).astype(F32)

    def packed_wet(pack):
        at = 2 * (kinds - 1)
        level = jnp.where(odd, pack[:, at + 1 : at + 2], pack[:, at : at + 1])
        return jnp.where(level_of < level, 1.0, 0.0)

    wet_own, wet_close, wet_far = packed_wet(own), packed_wet(close), packed_wet(far)
    firsts[...] = wet_close * (
        wet_own * (own - close)
        + wet_far * (far - close)
        + roll(wet_close, -1, 0) * (roll(close, -1, 0) - close)
        + roll(wet_close, 1, 0) * (roll(close, 1, 0) - close)
    )

    def sides(x, pack, k):
        rim = pltpu.roll(pack, cols - 1 - 2 * k, 1)
        lane = lanes(x.shape)
        return (
            jnp.where(lane == cols - 1, rim, roll(x, -1, 1)),
            jnp.where(lane == 0, rim, roll(x, 1, 1)),
        )

    whole = slice(PAD, top_row)
    northern = slice(PAD + 1, top_row + 1)
    southern = slice(PAD - 1, top_row - 1)
    for index in range(2):
        c = flats[index, whole, :]
        c_east, c_west = sides(c, near[1, whole, :], 4 * count + index)
        others = (c_east, c_west, flats[index, northern, :], flats[index, southern, :])
        for n, other in enumerate(others):
            faces[index, n, 0:rows, :] = 0.5 * (c + other)
    lev_east, lev_west = sides(flats[2], near[1], kinds - 1)
    faces[2, 0] = lev_east
    faces[2, 1] = lev_west

    wide = slice(PAD - 1, top_row + PAD - 1)
    wide_north = slice(PAD, top_row + PAD)
    wide_south = slice(PAD - 2, top_row + PAD - 2)

    def masks(level, here, north, south):
        return (
            level < flats[2, here, :],
            level < faces[2, 0, here, :],
            level < faces[2, 1, here, :],
            level < flats[2, north, :],
            level < flats[2, south, :],
        )

    def weighted(x, neighbours, wets, index):
        total = None
        for n, other in enumerate(neighbours):
            term = faces[index, n, 0:rows, :] * jnp.where(wets[n + 1], other - x, 0.0)
            total = term if total is None else total + term
        return total

    def velocity_level(level, carry):
        level_float = level.astype(F32)
        wets = masks(level_float, wide, wide_north, wide_south)
        for comp in range(2):
            k = comp * count + level
            x = fields[k, wide, :]
            x_east, x_west = sides(x, near[1, wide, :], k)
            first = (
                jnp.where(wets[1], x_east - x, 0.0)
                + jnp.where(wets[2], x_west - x, 0.0)
                + jnp.where(wets[3], fields[k, wide_north, :] - x, 0.0)
                + jnp.where(wets[4], fields[k, wide_south, :] - x, 0.0)
            )
            laps[comp, wide, :] = jnp.where(wets[0], first, 0.0)
        wets = masks(level_float, whole, northern, southern)
        for comp in range(2):
            k = comp * count + level
            x = laps[comp, whole, :]
            x_east, x_west = sides(x, firsts[whole, :], k)
            second = weighted(x, (x_east, x_west, laps[comp, northern, :], laps[comp, southern, :]), wets, 0)
            turned = faces[2, 2, 0:rows, :] * fields[(1 - comp) * count + level, whole, :]
            star = fields[k, whole, :] - second
            star = jnp.where(wets[0], star + turned if comp == 0 else star - turned, 0.0)
            star_out[k] = star
            deep[2 + comp, 0, start:stop, :] += star
        return carry

    lax.fori_loop(0, count, velocity_level, 0)

    levels_here = flats[2, whole, :]
    ocean_here = jnp.where(levels_here > 0, 1.0, 0.0)
    for comp in range(2):
        mean = deep[2 + comp, 0, start:stop, :] / jnp.maximum(levels_here, 1.0)
        extra_out[comp] = mean
        deep[2 + comp, 0, start:stop, :] = mean + wind[comp] * ocean_here

    def flow_edge(i):
        at = stop - DEEP if i == 0 else start
        return deep.at[2:4, 0, at : at + DEEP, :]

    fold_dst = lambda i: fold_recv.at[i]
    rows_out(flow_edge, fold_dst, 3)

    def tracer_level(level, carry):
        wets = masks(level.astype(F32), whole, northern, southern)
        for comp in range(2):
            k = 2 * count + comp * count + level
            x = fields[k, whole, :]
            x_east, x_west = sides(x, near[1, whole, :], k)
            change = weighted(x, (x_east, x_west, fields[k, northern, :], fields[k, southern, :]), wets, 1)
            tracer_out[comp * count + level] = x + jnp.where(wets[0], change, 0.0)
        return carry

    early = (3 * count) // 5
    lax.fori_loop(0, early, tracer_level, 0)

    rows_in(flow_edge, fold_dst, 3)

    @pl.when(top)
    def _():
        for comp in range(2):
            turned = -mirrored(fold_recv[0, comp])
            for n in range(DEEP):
                fold_recv[0, comp, n : n + 1, :] = turned[DEEP - 1 - n : DEEP - n]

    for comp in range(2):
        deep[2 + comp, 0, stop:end, :] = fold_recv[0, comp]

    @pl.when(jnp.logical_not(bottom))
    def _():
        for comp in range(2):
            deep[2 + comp, 0, PAD:start, :] = fold_recv[1, comp]

    for comp in range(2):
        pack_strips(1, comp)
    flow_copies = cols_copies(strip_send.at[1], strip_recv.at[1], 4)
    for copy in flow_copies:
        copy.start()

    for copy in stat_copies:
        copy.wait_recv()
    for f in range(2):
        unpack_strips(0, f)
    lax.fori_loop(early, count, tracer_level, 0)
    centre = slice(PAD, end)
    up = slice(PAD + 1, end + 1)
    down = slice(PAD - 1, end - 1)
    for tile in range(2):
        ocean[tile, centre, :] = jnp.where(deep[1, tile, centre, :] > 0, 1.0, 0.0)
    totals = [floor_diag * ocean[n, centre, :] + (1.0 - ocean[n, centre, :]) for n in range(2)]
    at = 0
    for where_from in (centre, up, down):
        d = [deep[0, n, where_from, :] for n in range(2)]
        o = [ocean[n, where_from, :] for n in range(2)]
        d_sides, o_sides = lane_sides(*d), lane_sides(*o)
        moved = [(d_sides[0], o_sides[0]), (d_sides[1], o_sides[1])]
        scale = 1.0 if where_from is centre else 0.5
        moved = [(scale, a, b) for a, b in moved]
        if where_from is not centre:
            moved.append((1.0, d, o))
        for scale, d_n, o_n in moved:
            for n in range(2):
                weight = scale * 0.5 * (deep[0, n, centre, :] + d_n[n]) * ocean[n, centre, :] * o_n[n]
                weights[at, n] = weight
                totals[n] = totals[n] + weight
            at += 1
    for n in range(2):
        weights[8, n] = totals[n]
        weights[9, n] = 0.5 * flow_step * ocean[n, centre, :]
        weights[10, n] = 0.5 * slope_step * ocean[n, centre, :]

    for copy in flow_copies:
        copy.wait_recv()
    for comp in range(2):
        unpack_strips(1, comp)
    rows_sent(flow_edge, fold_dst, 3)

    def subcycle(step, carry):
        flux_east = [deep[0, n, centre, :] * deep[2, n, centre, :] for n in range(2)]
        for n in range(2):
            flux[n, centre, :] = deep[0, n, centre, :] * deep[3, n, centre, :]
        easts, wests = lane_sides(*flux_east)
        high = []
        for n in range(2):
            divergence = (easts[n] - wests[n]) + (flux[n, up, :] - flux[n, down, :])
            high.append(basis[0, n, centre, :] - weights[9, n] * divergence)
            basis[0, n, centre, :] = high[n]
        easts, wests = lane_sides(*high)
        for n in range(2):
            slope = weights[10, n]
            deep[2, n, centre, :] = deep[2, n, centre, :] - slope * (easts[n] - wests[n])
            deep[3, n, centre, :] = deep[3, n, centre, :] - slope * (
                basis[0, n, up, :] - basis[0, n, down, :]
            )
        return carry

    lax.fori_loop(0, SUBCYCLES, subcycle, 0)

    for k in range(SOLVE_ITERS):
        summed = [(weights[8, n] - SHIFTS[k]) * basis[k, n, centre, :] for n in range(2)]
        at = 0
        for where_from in (centre, up, down):
            p = [basis[k, n, where_from, :] for n in range(2)]
            terms = list(lane_sides(*p)) + ([] if where_from is centre else [p])
            for term in terms:
                for n in range(2):
                    summed[n] = summed[n] - weights[at, n] * term[n]
                at += 1
        for n in range(2):
            basis[k + 1, n, centre, :] = summed[n] * (1.0 / SCALE)

    pairs = [(i, j) for i in range(SOLVE_ITERS) for j in range(i, SOLVE_ITERS + 1)]
    inside = [basis[k, 0, start:stop, :] for k in range(SOLVE_ITERS + 1)]
    lat_parts[...] = jnp.zeros(lat_parts.shape, F32)
    for n, (i, j) in enumerate(pairs):
        lat_parts[n : n + 1, :] = jnp.sum(inside[i] * inside[j], axis=0, keepdims=True)

    def all_sum(parts, slots, sends, recvs, axis, me, size):
        copies = [
            remote(parts, slots.at[d - 1], sends.at[d - 1], recvs.at[d - 1], {axis: lax.rem(me + d, size)})
            for d in range(1, size)
        ]
        for copy in copies:
            copy.start()
        for copy in copies:
            copy.wait()
        result = parts[...]
        for d in range(1, size):
            result = result + slots[d - 1]
        return result

    lon_parts[...] = all_sum(lat_parts, lat_sums, lat_send, lat_recv, "lat", lat, n_lat)
    sums = jnp.sum(
        all_sum(lon_parts, lon_sums, lon_send, lon_recv, "lon", lon, n_lon), axis=1, keepdims=True
    )
    gram = {}
    for n, (i, j) in enumerate(pairs):
        gram[i, j] = gram[j, i] = sums[n : n + 1, :]

    def inner_product(a, b):
        result = None
        for i, x in a.items():
            for j, y in b.items():
                term = x * y * gram[i, j]
                result = term if result is None else result + term
        return result

    def image_of(a):
        result = {}
        for n, x in a.items():
            for at, value in ((n, SHIFTS[n] * x), (n + 1, SCALE * x)):
                result[at] = result[at] + value if at in result else value
        return result

    one = jnp.ones((1, 1), F32)
    residual = {0: one}
    direction = {0: one}
    answer = {}
    norm = gram[0, 0]
    for iteration in range(SOLVE_ITERS):
        image = image_of(direction)
        step = norm / inner_product(direction, image)
        for n, x in direction.items():
            answer[n] = answer[n] + step * x if n in answer else step * x
        if iteration < SOLVE_ITERS - 1:
            residual = {n: (residual[n] if n in residual else 0.0) - step * x for n, x in image.items()}
            new_norm = inner_product(residual, residual)
            ratio = new_norm / norm
            direction = {
                n: x + ratio * direction[n] if n in direction else x for n, x in residual.items()
            }
            norm = new_norm
    for tile in range(2):
        surface = None
        for n, x in answer.items():
            term = x * basis[n, tile, centre, :]
            surface = term if surface is None else surface + term
        flux[tile, centre, :] = surface

    easts, wests = lane_sides(flux[0, start:stop, :], flux[1, start:stop, :])
    slopes = (easts[0] - wests[0], flux[0, start + 1 : stop + 1, :] - flux[0, start - 1 : stop - 1, :])
    for comp, slope in enumerate(slopes):
        final = deep[2 + comp, 0, start:stop, :] - weights[10, 0, DEEP : DEEP + rows, :] * slope
        extra_out[comp] = final - extra_out[comp]
    extra_out[2] = levels_here
    extra_out[3] = flux[0, start:stop, :]
    rows_sent(row_src, row_dst, 0)
    for copy in col_copies + stat_copies + flow_copies:
        copy.wait_send()


def finish(tracer_ref, star_ref, extra_ref, tracer_out, velocity_out, surface_out, corrected, sems):
    count = star_ref.shape[0] // 2
    copies = [
        pltpu.make_async_copy(tracer_ref, tracer_out, sems.at[0]),
        pltpu.make_async_copy(extra_ref.at[3], surface_out, sems.at[1]),
    ]
    for copy in copies:
        copy.start()
    for comp in range(2):

        def correct(level, carry):
            k = comp * count + level
            wet = level.astype(F32) < extra_ref[2]
            corrected[k] = star_ref[k] + jnp.where(wet, extra_ref[comp], 0.0)
            return carry

        lax.fori_loop(0, count, correct, 0)
        part = slice(comp * count, (comp + 1) * count)
        copies.append(pltpu.make_async_copy(corrected.at[part], velocity_out.at[part], sems.at[2 + comp]))
        copies[-1].start()
    for copy in copies:
        copy.wait()


def per_device(n_lon, n_lat, tracers, velocity, active_levels, diffusivity, viscosity, ocean_depth, wind_forcing):
    _, count, rows, cols = tracers.shape
    kinds = 4 * count + 3
    packed = -(-2 * kinds // 8) * 8
    message = packed + 2 * DEEP
    tall, deep_rows = rows + 2 * PAD, rows + 2 * DEEP
    padded = deep_rows + 2 * PAD
    strip_rows = 8 * -(-(deep_rows // 8) // (cols // STRIP))
    entries = 16
    block = jax.ShapeDtypeStruct((2 * count, rows, cols), F32)
    flat = jax.ShapeDtypeStruct((rows, cols), F32)
    vmem = pl.BlockSpec(memory_space=pltpu.VMEM)
    hbm = pl.BlockSpec(memory_space=pltpu.HBM)
    out = pl.pallas_call(
        functools.partial(kernel, n_lon, n_lat),
        out_shape=(block, block, jax.ShapeDtypeStruct((4, rows, cols), F32)),
        in_specs=[hbm] * 7,
        out_specs=(vmem, vmem, vmem),
        scratch_shapes=[
            pltpu.VMEM((4 * count, tall, cols), F32),
            pltpu.VMEM((3, tall, cols), F32),
            pltpu.VMEM((rows, cols), jnp.int32),
            pltpu.VMEM((2, rows, cols), F32),
            pltpu.VMEM((2, tall, cols), F32),
            pltpu.VMEM((tall, cols), F32),
            pltpu.VMEM((2, tall, cols), F32),
            pltpu.VMEM((3, 4, tall, cols), F32),
            pltpu.VMEM((4, 2, padded, cols), F32),
            pltpu.VMEM((2, padded, cols), F32),
            pltpu.VMEM((11, 2, deep_rows, cols), F32),
            pltpu.VMEM((2, padded, cols), F32),
            pltpu.VMEM((SOLVE_ITERS + 1, 2, padded, cols), F32),
            pltpu.VMEM((2, message, cols), F32),
            pltpu.VMEM((2, message, cols), F32),
            pltpu.VMEM((2, tall, cols), F32),
            pltpu.VMEM((2, tall, cols), F32),
            pltpu.VMEM((2, 2, 2, strip_rows, cols), F32),
            pltpu.VMEM((2, 2, 2, strip_rows, cols), F32),
            pltpu.VMEM((2, 2, DEEP, cols), F32),
            pltpu.VMEM((n_lat - 1, entries, cols), F32),
            pltpu.VMEM((n_lon - 1, entries, cols), F32),
            pltpu.VMEM((entries, cols), F32),
            pltpu.VMEM((entries, cols), F32),
            pltpu.SemaphoreType.DMA((7,)),
            pltpu.SemaphoreType.DMA((5, 2)),
            pltpu.SemaphoreType.DMA((5, 2)),
            pltpu.SemaphoreType.DMA((n_lat - 1,)),
            pltpu.SemaphoreType.DMA((n_lat - 1,)),
            pltpu.SemaphoreType.DMA((n_lon - 1,)),
            pltpu.SemaphoreType.DMA((n_lon - 1,)),
        ],
        compiler_params=pltpu.CompilerParams(
            collective_id=0, has_side_effects=True, vmem_limit_bytes=32 * 1024 * 1024
        ),
    )(
        tracers.reshape(2 * count, rows, cols),
        velocity.reshape(2 * count, rows, cols),
        active_levels,
        diffusivity,
        viscosity,
        ocean_depth,
        wind_forcing,
    )
    out = pl.pallas_call(
        finish,
        out_shape=(block, block, flat),
        in_specs=[vmem] * 3,
        out_specs=(hbm, hbm, hbm),
        scratch_shapes=[pltpu.VMEM((2 * count, rows, cols), F32), pltpu.SemaphoreType.DMA((4,))],
        compiler_params=pltpu.CompilerParams(vmem_limit_bytes=16 * 1024 * 1024),
    )(*out)
    return out[0].reshape(tracers.shape), out[1].reshape(velocity.shape), out[2]


def solution(mesh):
    flat = P("lat", "lon")
    deep = P(None, None, "lat", "lon")
    return jax.shard_map(
        functools.partial(per_device, mesh.shape["lon"], mesh.shape["lat"]),
        mesh=mesh,
        in_specs=(deep, deep, flat, flat, flat, flat, P(None, "lat", "lon")),
        out_specs=(deep, deep, flat),
        check_vma=False,
    )
```

```python
import functools
import math

import jax
import jax.numpy as jnp
from jax import lax
from jax.experimental import pallas as pl
from jax.experimental.pallas import tpu as pltpu
from jax.sharding import PartitionSpec as P

SUBCYCLES = 8
SOLVE_ITERS = 4
flow_step = 0.3
slope_step = 0.3
floor_diag = 0.05

PAD = 8
DEEP = 24
STRIP = 32
MESH = pl.DeviceIdType.MESH
F32 = jnp.float32

SHIFTS = (0.0, 5.0, 2.5, 8.0)
SCALE = 5.0


def roll(x, shift, axis):
    return pltpu.roll(x, shift % x.shape[axis], axis)


def lanes(shape):
    return lax.broadcasted_iota(jnp.int32, shape, len(shape) - 1)


def lane_sides(a, b):
    cols = a.shape[-1]
    lane = lanes(a.shape)
    last, first = lane == cols - 1, lane == 0
    a_up, b_up = roll(a, -1, 1), roll(b, -1, 1)
    a_down, b_down = roll(a, 1, 1), roll(b, 1, 1)
    east = (jnp.where(last, b_up, a_up), jnp.where(last, a_up, b_up))
    west = (jnp.where(first, b_down, a_down), jnp.where(first, a_down, b_down))
    return east, west


def mirrored(x):
    return jnp.take_along_axis(x, x.shape[1] - 1 - lanes(x.shape), axis=1)


def upturned(x):
    ids = 7 - lax.broadcasted_iota(jnp.int32, (8, x.shape[1]), 0)
    tiles = [x[at : at + 8] for at in range(0, x.shape[0], 8)]
    return jnp.concatenate([jnp.take_along_axis(tile, ids, axis=0) for tile in tiles[::-1]], axis=0)


def folded(x):
    return upturned(mirrored(x))


def kernel(
    n_lon,
    n_lat,
    tracer_hbm,
    velocity_hbm,
    levels_hbm,
    diff_hbm,
    visc_hbm,
    depth_hbm,
    wind_hbm,
    tracer_hbm_out,
    star_hbm_out,
    extra_hbm_out,
    tracer_out,
    star_out,
    extra_out,
    fields,
    flats,
    levels_in,
    wind,
    near,
    firsts,
    laps,
    faces,
    deep,
    ocean,
    weights,
    flux,
    basis,
    row_send,
    row_recv,
    col_send,
    col_recv,
    strip_send,
    strip_recv,
    corner_send,
    corner_recv,
    fold_recv,
    part,
    parts,
    load_sems,
    store_sems,
    send_sems,
    recv_sems,
    corner_send_sems,
    corner_recv_sems,
    sum_send,
    sum_recv,
):
    count = tracer_hbm.shape[0] // 2
    rows, cols = levels_hbm.shape
    top_row = PAD + rows
    deep_rows = rows + 2 * DEEP
    start = PAD + DEEP
    stop = start + rows
    end = PAD + deep_rows
    lon = lax.axis_index("lon")
    lat = lax.axis_index("lat")
    right = lax.rem(lon + 1, n_lon)
    left = lax.rem(lon + n_lon - 1, n_lon)
    mirror = n_lon - 1 - lon
    top = lat == n_lat - 1
    bottom = lat == 0
    above = jnp.minimum(lat + 1, n_lat - 1)
    below = jnp.maximum(lat - 1, 0)

    loads = [
        pltpu.make_async_copy(src, dst, load_sems.at[n])
        for n, (src, dst) in enumerate(
            (
                (velocity_hbm, fields.at[0 : 2 * count, PAD:top_row, :]),
                (tracer_hbm, fields.at[2 * count : 4 * count, PAD:top_row, :]),
                (levels_hbm, levels_in),
                (visc_hbm, flats.at[0, PAD:top_row, :]),
                (diff_hbm, flats.at[1, PAD:top_row, :]),
                (depth_hbm, deep.at[0, 0, start:stop, :]),
                (wind_hbm, wind),
            )
        )
    ]
    for load in loads:
        load.start()

    def remote(src, dst, send, recv, device):
        return pltpu.make_async_remote_copy(
            src_ref=src, dst_ref=dst, send_sem=send, recv_sem=recv, device_id=device, device_id_type=MESH
        )

    barrier = pltpu.get_barrier_semaphore()

    def peer(k):
        return {
            "lat": lax.rem(lat + k // n_lon, n_lat),
            "lon": lax.rem(lon + lax.rem(k, n_lon), n_lon),
        }

    def greet(k, carry):
        pl.semaphore_signal(barrier, inc=1, device_id=peer(k), device_id_type=MESH)
        return carry

    lax.fori_loop(1, n_lon * n_lat, greet, 0)

    kinds = 4 * count + 3
    packed = -(-2 * kinds // 8) * 8
    row_send[:, 2 * kinds : packed, :] = jnp.zeros((2, packed - 2 * kinds, cols), F32)
    deep[2:4] = jnp.zeros((2,) + deep.shape[1:], F32)
    for array in (flux, ocean):
        array[:, 0:PAD, :] = jnp.zeros((2, PAD, cols), F32)
        array[:, end:, :] = jnp.zeros((2, PAD, cols), F32)
    for array in (basis, deep.at[0:2]):
        array[:, :, 0:PAD, :] = jnp.zeros((array.shape[0], 2, PAD, cols), F32)
        array[:, :, end:, :] = jnp.zeros((array.shape[0], 2, PAD, cols), F32)
    basis[0, :, PAD:end, :] = jnp.zeros((2, deep_rows, cols), F32)
    laps[...] = jnp.zeros(laps.shape, F32)
    @pl.when(bottom)
    def _():
        row_recv[1] = jnp.zeros(row_recv.shape[1:], F32)
        corner_recv[:, 2:4] = jnp.zeros((2, 2) + corner_recv.shape[2:], F32)

    for load in loads:
        load.wait()

    levels_float = levels_in[...].astype(F32)
    flats[2, PAD:top_row, :] = levels_float
    deep[1, 0, start:stop, :] = levels_float

    def block_of(k):
        return (fields, k) if k < 4 * count else (flats, k - 4 * count)

    for k in range(kinds):
        ref, index = block_of(k)
        row_send[0, 2 * k : 2 * k + 2, :] = ref[index, top_row - 2 : top_row, :]
        row_send[1, 2 * k : 2 * k + 1, :] = ref[index, PAD + 1 : PAD + 2, :]
        row_send[1, 2 * k + 1 : 2 * k + 2, :] = ref[index, PAD : PAD + 1, :]
    for f in range(2):
        at = packed + f * DEEP
        row_send[0, at : at + DEEP, :] = deep[f, 0, stop - DEEP : stop, :]
        row_send[1, at : at + DEEP, :] = deep[f, 0, start : start + DEEP, :]

    pl.semaphore_wait(barrier, n_lon * n_lat - 1)

    def rows_out(src, dst, stage):
        @pl.when(top)
        def _():
            remote(src(0), dst(0), send_sems.at[stage, 0], recv_sems.at[stage, 0], {"lon": mirror}).start()

        @pl.when(jnp.logical_not(top))
        def _():
            remote(src(0), dst(1), send_sems.at[stage, 0], recv_sems.at[stage, 1], {"lat": above}).start()

        @pl.when(jnp.logical_not(bottom))
        def _():
            remote(src(1), dst(0), send_sems.at[stage, 1], recv_sems.at[stage, 0], {"lat": below}).start()

    def rows_in(src, dst, stage):
        remote(src(0), dst(0), send_sems.at[stage, 0], recv_sems.at[stage, 0], {"lat": above}).wait_recv()

        @pl.when(jnp.logical_not(bottom))
        def _():
            remote(src(1), dst(1), send_sems.at[stage, 1], recv_sems.at[stage, 1], {"lat": below}).wait_recv()

    def rows_sent(src, dst, stage):
        remote(src(0), dst(0), send_sems.at[stage, 0], recv_sems.at[stage, 0], {"lat": above}).wait_send()

        @pl.when(jnp.logical_not(bottom))
        def _():
            remote(src(1), dst(1), send_sems.at[stage, 1], recv_sems.at[stage, 1], {"lat": below}).wait_send()

    def cols_copies(send, recv, stage):
        return (
            remote(send.at[0], recv.at[0], send_sems.at[stage, 0], recv_sems.at[stage, 0], {"lon": right}),
            remote(send.at[1], recv.at[1], send_sems.at[stage, 1], recv_sems.at[stage, 1], {"lon": left}),
        )

    row_src = lambda i: row_send.at[i]
    row_dst = lambda i: row_recv.at[i]
    rows_out(row_src, row_dst, 0)

    lane = lanes((rows, cols))
    own = jnp.zeros((rows, cols), F32)
    inner = jnp.zeros((rows, cols), F32)
    odd_here = jnp.bitwise_and(lane, 1) == 1
    for k in range(kinds):
        ref, index = block_of(k)
        x = ref[index, PAD:top_row, :]
        pair = jnp.right_shift(lane, 1) == k
        own = jnp.where(pair, roll(x, 2 * k + 1, 1), own)
        if k < 2 * count or k == kinds - 1:
            inner = jnp.where(pair, jnp.where(odd_here, roll(x, 2 * k, 1), roll(x, 2 * k + 2, 1)), inner)
    col_send[1] = jnp.where(odd_here, own, roll(inner, -1, 1))
    col_send[0] = jnp.where(odd_here, roll(inner, 1, 1), own)
    col_copies = cols_copies(col_send, col_recv, 1)
    for copy in col_copies:
        copy.start()

    groups = cols // STRIP
    tiles = rows // 8
    rim_tiles = DEEP // 8
    group_of = lanes((8, cols)) // STRIP

    def strip_of(ref, base, first_row, number):
        strip = None
        for g in range(number):
            at = first_row + 8 * g
            x = roll(ref[at : at + 8, :], STRIP * g - base, 1)
            strip = x if strip is None else jnp.where(group_of == g, x, strip)
        return strip

    def pack_strips(pair, f):
        ref = deep.at[2 * pair + f, 0]
        for side, base in ((0, cols - STRIP), (1, 0)):
            for t in range(0, tiles, groups):
                at = 8 * (t // groups)
                strip_send[pair, side, f, at : at + 8, :] = strip_of(
                    ref, base, start + 8 * t, min(groups, tiles - t)
                )
            for corner, first_row in ((side, stop - DEEP), (2 + side, start)):
                corner_send[pair, corner, 8 * f : 8 * f + 8, :] = strip_of(ref, base, first_row, rim_tiles)

    def fill(pair, f, at, west_tile, east_tile, g):
        low = roll(east_tile, -STRIP * g, 1)
        high = roll(west_tile, cols - STRIP - STRIP * g, 1)
        deep[2 * pair + f, 1, at : at + 8, :] = jnp.where(group_of < groups // 2, low, high)

    def unpack_strips(pair, f, sign):
        for j in range(tiles):
            at = 8 * (j // groups)
            west_tile = strip_recv[pair, 0, f, at : at + 8, :]
            east_tile = strip_recv[pair, 1, f, at : at + 8, :]
            fill(pair, f, start + 8 * j, west_tile, east_tile, j % groups)
        tile_at = slice(8 * f, 8 * f + 8)

        @pl.when(top)
        def _():
            for corner in range(2):
                tile = folded(corner_recv[pair, corner, tile_at, :])
                corner_recv[pair, corner, tile_at, :] = sign * roll(tile, -STRIP, 1)

        for j in range(rim_tiles):
            fill(pair, f, stop + 8 * j, corner_recv[pair, 1, tile_at, :], corner_recv[pair, 0, tile_at, :], j)
            fill(
                pair, f, PAD + 8 * j, corner_recv[pair, 3, tile_at, :], corner_recv[pair, 2, tile_at, :], j
            )

    turned_lon = (lax.rem(2 * n_lon - 2 - lon, n_lon), lax.rem(n_lon - lon, n_lon))
    alone = [jnp.logical_and(top, turned == lon) for turned in turned_lon]

    def corner_copy(pair, corner, slot, device):
        size = 24 if pair == 0 else 16
        return remote(
            corner_send.at[pair, corner, 0:size, :],
            corner_recv.at[pair, slot, 0:size, :],
            corner_send_sems.at[pair, corner],
            corner_recv_sems.at[pair, slot],
            device,
        )

    def corners_out(pair):
        for corner in range(2):
            side = right if corner == 0 else left

            @pl.when(jnp.logical_not(top))
            def _():
                corner_copy(pair, corner, 3 - corner, {"lat": above, "lon": side}).start()

            @pl.when(jnp.logical_and(top, turned_lon[corner] != lon))
            def _():
                corner_copy(pair, corner, corner, {"lon": turned_lon[corner]}).start()

            @pl.when(alone[corner])
            def _():
                corner_recv[pair, corner] = corner_send[pair, corner]

            @pl.when(jnp.logical_not(bottom))
            def _():
                corner_copy(pair, 2 + corner, 1 - corner, {"lat": below, "lon": side}).start()

    def corners_each(pair, act):
        for corner in range(2):
            side = right if corner == 0 else left

            @pl.when(jnp.logical_not(alone[corner]))
            def _():
                act(corner_copy(pair, corner, corner, {"lat": above, "lon": side}))

            @pl.when(jnp.logical_not(bottom))
            def _():
                act(corner_copy(pair, 2 + corner, 2 + corner, {"lat": below, "lon": side}))

    for corner in range(4):
        at = rows - 8 if corner < 2 else 0
        corner_send[0, corner, 16:24, :] = own[at : at + 8]
    for f in range(2):
        pack_strips(0, f)
    corners_out(0)
    stat_copies = cols_copies(strip_send.at[0], strip_recv.at[0], 2)
    for copy in stat_copies:
        copy.start()

    row_ids = (lat * rows + lax.broadcasted_iota(jnp.int32, (rows, cols), 0)).astype(F32)
    coriolis = 0.25 * jnp.sin(math.pi * ((row_ids + 0.5) / (rows * n_lat) - 0.5))
    faces[2, 2, 0:rows, :] = coriolis

    rows_in(row_src, row_dst, 0)

    @pl.when(top)
    def _():
        turned = mirrored(row_recv[0])
        ids = lax.broadcasted_iota(jnp.int32, turned.shape, 0)
        turned = jnp.where(ids < 4 * count, -turned, turned)
        row_recv[0, 0:packed, :] = turned[0:packed]
        for f in range(2):
            at = packed + f * DEEP
            row_recv[0, at : at + DEEP, :] = upturned(turned[at : at + DEEP])

    for f in range(2):
        at = packed + f * DEEP
        deep[f, 0, PAD:start, :] = row_recv[1, at : at + DEEP, :]
        deep[f, 0, stop:end, :] = row_recv[0, at : at + DEEP, :]

    for k in range(kinds):
        ref, index = block_of(k)
        ref[index, top_row : top_row + 1, :] = row_recv[0, 2 * k + 1 : 2 * k + 2, :]
        ref[index, top_row + 1 : top_row + 2, :] = row_recv[0, 2 * k : 2 * k + 1, :]
        ref[index, PAD - 2 : PAD, :] = row_recv[1, 2 * k : 2 * k + 2, :]

    for copy in col_copies:
        copy.wait_recv()
    corners_each(0, lambda copy: copy.wait_recv())
    tall = rows + 2 * PAD
    lane = lanes((tall, cols))
    odd = jnp.bitwise_and(lane, 1) == 1
    from_west, from_east = col_recv[0], col_recv[1]
    near[1] = jnp.zeros((tall, cols), F32)
    near[0] = jnp.zeros((tall, cols), F32)
    near[1, PAD:top_row, :] = jnp.where(odd_here, roll(from_west, 1, 1), roll(from_east, -1, 1))
    near[0, PAD:top_row, :] = jnp.where(odd_here, from_west, from_east)
    odd_tile = jnp.bitwise_and(lanes((8, cols)), 1) == 1
    ne, nw, se, sw = [corner_recv[0, corner, 16:24, :] for corner in range(4)]
    below_tile = jnp.where(odd_tile, roll(sw, 1, 1), roll(se, -1, 1))
    near[1, PAD - 1 : PAD, :] = below_tile[7:8]

    @pl.when(top)
    def _():
        tile = jnp.where(odd_tile, nw, ne)
        tile = jnp.where(lanes((8, cols)) < 4 * count, -tile, tile)
        near[1, top_row : top_row + 1, :] = tile[7:8]

    @pl.when(jnp.logical_not(top))
    def _():
        tile = jnp.where(odd_tile, roll(nw, 1, 1), roll(ne, -1, 1))
        near[1, top_row : top_row + 1, :] = tile[0:1]

    close, far = near[1], near[0]
    own = jnp.concatenate([jnp.zeros((PAD, cols), F32), own, jnp.zeros((PAD, cols), F32)], axis=0)

    level_of = lax.rem(jnp.right_shift(lane, 1), count).astype(F32)

    def packed_wet(pack):
        at = 2 * (kinds - 1)
        level = jnp.where(odd, pack[:, at + 1 : at + 2], pack[:, at : at + 1])
        return jnp.where(level_of < level, 1.0, 0.0)

    wet_own, wet_close, wet_far = packed_wet(own), packed_wet(close), packed_wet(far)
    firsts[...] = wet_close * (
        wet_own * (own - close)
        + wet_far * (far - close)
        + roll(wet_close, -1, 0) * (roll(close, -1, 0) - close)
        + roll(wet_close, 1, 0) * (roll(close, 1, 0) - close)
    )

    def sides(x, pack, k):
        rim = pltpu.roll(pack, cols - 1 - 2 * k, 1)
        lane = lanes(x.shape)
        return (
            jnp.where(lane == cols - 1, rim, roll(x, -1, 1)),
            jnp.where(lane == 0, rim, roll(x, 1, 1)),
        )

    whole = slice(PAD, top_row)
    northern = slice(PAD + 1, top_row + 1)
    southern = slice(PAD - 1, top_row - 1)
    for index in range(2):
        c = flats[index, whole, :]
        c_east, c_west = sides(c, near[1, whole, :], 4 * count + index)
        others = (c_east, c_west, flats[index, northern, :], flats[index, southern, :])
        for n, other in enumerate(others):
            faces[index, n, 0:rows, :] = 0.5 * (c + other)
    lev_east, lev_west = sides(flats[2], near[1], kinds - 1)
    faces[2, 0] = lev_east
    faces[2, 1] = lev_west

    wide = slice(PAD - 1, top_row + PAD - 1)
    wide_north = slice(PAD, top_row + PAD)
    wide_south = slice(PAD - 2, top_row + PAD - 2)

    def masks(level, here, north, south):
        return (
            level < flats[2, here, :],
            level < faces[2, 0, here, :],
            level < faces[2, 1, here, :],
            level < flats[2, north, :],
            level < flats[2, south, :],
        )

    def weighted(x, neighbours, wets, index):
        total = None
        for n, other in enumerate(neighbours):
            term = faces[index, n, 0:rows, :] * jnp.where(wets[n + 1], other - x, 0.0)
            total = term if total is None else total + term
        return total

    def velocity_level(level, carry):
        level_float = level.astype(F32)
        wets = masks(level_float, wide, wide_north, wide_south)
        for comp in range(2):
            k = comp * count + level
            x = fields[k, wide, :]
            x_east, x_west = sides(x, near[1, wide, :], k)
            first = (
                jnp.where(wets[1], x_east - x, 0.0)
                + jnp.where(wets[2], x_west - x, 0.0)
                + jnp.where(wets[3], fields[k, wide_north, :] - x, 0.0)
                + jnp.where(wets[4], fields[k, wide_south, :] - x, 0.0)
            )
            laps[comp, wide, :] = jnp.where(wets[0], first, 0.0)
        wets = masks(level_float, whole, northern, southern)
        for comp in range(2):
            k = comp * count + level
            x = laps[comp, whole, :]
            x_east, x_west = sides(x, firsts[whole, :], k)
            second = weighted(x, (x_east, x_west, laps[comp, northern, :], laps[comp, southern, :]), wets, 0)
            turned = faces[2, 2, 0:rows, :] * fields[(1 - comp) * count + level, whole, :]
            star = fields[k, whole, :] - second
            star = jnp.where(wets[0], star + turned if comp == 0 else star - turned, 0.0)
            star_out[k] = star
            deep[2 + comp, 0, start:stop, :] += star
        return carry

    lax.fori_loop(0, count, velocity_level, 0)

    levels_here = flats[2, whole, :]
    ocean_here = jnp.where(levels_here > 0, 1.0, 0.0)
    for comp in range(2):
        mean = deep[2 + comp, 0, start:stop, :] / jnp.maximum(levels_here, 1.0)
        extra_out[comp] = mean
        deep[2 + comp, 0, start:stop, :] = mean + wind[comp] * ocean_here

    def flow_edge(i):
        at = stop - DEEP if i == 0 else start
        return deep.at[2:4, 0, at : at + DEEP, :]

    fold_dst = lambda i: fold_recv.at[i]
    rows_out(flow_edge, fold_dst, 3)
    for comp in range(2):
        pack_strips(1, comp)
    flow_copies = cols_copies(strip_send.at[1], strip_recv.at[1], 4)
    for copy in flow_copies:
        copy.start()
    corners_out(1)
    stores = [pltpu.make_async_copy(star_out, star_hbm_out, store_sems.at[0])]
    stores[0].start()

    def tracer_level(level, carry):
        wets = masks(level.astype(F32), whole, northern, southern)
        for comp in range(2):
            k = 2 * count + comp * count + level
            x = fields[k, whole, :]
            x_east, x_west = sides(x, near[1, whole, :], k)
            change = weighted(x, (x_east, x_west, fields[k, northern, :], fields[k, southern, :]), wets, 1)
            tracer_out[comp * count + level] = x + jnp.where(wets[0], change, 0.0)
        return carry

    lax.fori_loop(0, count, tracer_level, 0)
    stores.append(pltpu.make_async_copy(tracer_out, tracer_hbm_out, store_sems.at[1]))
    stores[1].start()

    for copy in stat_copies:
        copy.wait_recv()
    for f in range(2):
        unpack_strips(0, f, 1.0)
    centre = slice(PAD, end)
    up = slice(PAD + 1, end + 1)
    down = slice(PAD - 1, end - 1)
    for tile in range(2):
        ocean[tile, centre, :] = jnp.where(deep[1, tile, centre, :] > 0, 1.0, 0.0)
    totals = [floor_diag * ocean[n, centre, :] + (1.0 - ocean[n, centre, :]) for n in range(2)]
    at = 0
    for where_from in (centre, up, down):
        d = [deep[0, n, where_from, :] for n in range(2)]
        o = [ocean[n, where_from, :] for n in range(2)]
        d_sides, o_sides = lane_sides(*d), lane_sides(*o)
        moved = [(d_sides[0], o_sides[0]), (d_sides[1], o_sides[1])]
        scale = 1.0 if where_from is centre else 0.5
        moved = [(scale, a, b) for a, b in moved]
        if where_from is not centre:
            moved.append((1.0, d, o))
        for scale, d_n, o_n in moved:
            for n in range(2):
                weight = scale * 0.5 * (deep[0, n, centre, :] + d_n[n]) * ocean[n, centre, :] * o_n[n]
                weights[at, n] = weight
                totals[n] = totals[n] + weight
            at += 1
    for n in range(2):
        weights[8, n] = totals[n]
        weights[9, n] = 0.5 * flow_step * ocean[n, centre, :]
        weights[10, n] = 0.5 * slope_step * ocean[n, centre, :]

    for copy in flow_copies:
        copy.wait_recv()
    corners_each(1, lambda copy: copy.wait_recv())
    rows_in(flow_edge, fold_dst, 3)
    for comp in range(2):
        unpack_strips(1, comp, -1.0)

    @pl.when(top)
    def _():
        for comp in range(2):
            fold_recv[0, comp] = -folded(fold_recv[0, comp])

    for comp in range(2):
        deep[2 + comp, 0, stop:end, :] = fold_recv[0, comp]

    @pl.when(jnp.logical_not(bottom))
    def _():
        for comp in range(2):
            deep[2 + comp, 0, PAD:start, :] = fold_recv[1, comp]

    rows_sent(flow_edge, fold_dst, 3)

    def subcycle(step, carry):
        flux_east = [deep[0, n, centre, :] * deep[2, n, centre, :] for n in range(2)]
        for n in range(2):
            flux[n, centre, :] = deep[0, n, centre, :] * deep[3, n, centre, :]
        easts, wests = lane_sides(*flux_east)
        high = []
        for n in range(2):
            divergence = (easts[n] - wests[n]) + (flux[n, up, :] - flux[n, down, :])
            high.append(basis[0, n, centre, :] - weights[9, n] * divergence)
            basis[0, n, centre, :] = high[n]
        easts, wests = lane_sides(*high)
        for n in range(2):
            slope = weights[10, n]
            deep[2, n, centre, :] = deep[2, n, centre, :] - slope * (easts[n] - wests[n])
            deep[3, n, centre, :] = deep[3, n, centre, :] - slope * (
                basis[0, n, up, :] - basis[0, n, down, :]
            )
        return carry

    lax.fori_loop(0, SUBCYCLES, subcycle, 0)

    for k in range(SOLVE_ITERS):
        summed = [(weights[8, n] - SHIFTS[k]) * basis[k, n, centre, :] for n in range(2)]
        at = 0
        for where_from in (centre, up, down):
            p = [basis[k, n, where_from, :] for n in range(2)]
            terms = list(lane_sides(*p)) + ([] if where_from is centre else [p])
            for term in terms:
                for n in range(2):
                    summed[n] = summed[n] - weights[at, n] * term[n]
                at += 1
        for n in range(2):
            basis[k + 1, n, centre, :] = summed[n] * (1.0 / SCALE)

    pairs = [(i, j) for i in range(SOLVE_ITERS) for j in range(i, SOLVE_ITERS + 1)]
    inside = [basis[k, 0, start:stop, :] for k in range(SOLVE_ITERS + 1)]
    lane_row = lanes((1, cols))
    packed_sums = jnp.zeros((1, cols), F32)
    for n, (i, j) in enumerate(pairs):
        value = jnp.sum(jnp.sum(inside[i] * inside[j], axis=0, keepdims=True), axis=1, keepdims=True)
        packed_sums = jnp.where(lane_row == n, value, packed_sums)
    me = lat * n_lon + lon
    part[0] = packed_sums
    parts[me] = packed_sums

    def sum_copy(k):
        return remote(part, parts.at[pl.ds(me, 1)], sum_send.at[k], sum_recv.at[k], peer(k))

    def sum_start(k, carry):
        sum_copy(k).start()
        return carry

    def sum_wait(k, carry):
        sum_copy(k).wait()
        return carry

    lax.fori_loop(1, n_lon * n_lat, sum_start, 0)
    lax.fori_loop(1, n_lon * n_lat, sum_wait, 0)
    sums = parts[0]
    for n in range(1, n_lon * n_lat):
        sums = sums + parts[n]
    sums = jnp.broadcast_to(sums, (8, cols))
    gram = {}
    for n, (i, j) in enumerate(pairs):
        gram[i, j] = gram[j, i] = jnp.broadcast_to(sums[:, n : n + 1], (8, cols))

    def inner_product(a, b):
        result = None
        for i, x in a.items():
            for j, y in b.items():
                term = x * y * gram[i, j]
                result = term if result is None else result + term
        return result

    def image_of(a):
        result = {}
        for n, x in a.items():
            for at, value in ((n, SHIFTS[n] * x), (n + 1, SCALE * x)):
                result[at] = result[at] + value if at in result else value
        return result

    one = jnp.ones((8, cols), F32)
    residual = {0: one}
    direction = {0: one}
    answer = {}
    norm = gram[0, 0]
    for iteration in range(SOLVE_ITERS):
        image = image_of(direction)
        step = norm / inner_product(direction, image)
        for n, x in direction.items():
            answer[n] = answer[n] + step * x if n in answer else step * x
        if iteration < SOLVE_ITERS - 1:
            residual = {n: (residual[n] if n in residual else 0.0) - step * x for n, x in image.items()}
            new_norm = inner_product(residual, residual)
            ratio = new_norm / norm
            direction = {
                n: x + ratio * direction[n] if n in direction else x for n, x in residual.items()
            }
            norm = new_norm
    for tile in range(2):
        surface = None
        for n, x in answer.items():
            term = x[0:1] * basis[n, tile, centre, :]
            surface = term if surface is None else surface + term
        flux[tile, centre, :] = surface

    easts, wests = lane_sides(flux[0, start:stop, :], flux[1, start:stop, :])
    slopes = (easts[0] - wests[0], flux[0, start + 1 : stop + 1, :] - flux[0, start - 1 : stop - 1, :])
    for comp, slope in enumerate(slopes):
        final = deep[2 + comp, 0, start:stop, :] - weights[10, 0, DEEP : DEEP + rows, :] * slope
        extra_out[comp] = final - extra_out[comp]
    extra_out[2] = levels_here
    extra_out[3] = flux[0, start:stop, :]
    stores.append(pltpu.make_async_copy(extra_out, extra_hbm_out, store_sems.at[2]))
    stores[2].start()
    rows_sent(row_src, row_dst, 0)
    for pair in range(2):
        corners_each(pair, lambda copy: copy.wait_send())
    for copy in col_copies + stat_copies + flow_copies:
        copy.wait_send()
    for store in stores:
        store.wait()


def finish(
    tracer_hbm, star_hbm, extra_hbm, tracer_out, velocity_out, surface_out, tracer, star, extra, corrected, sems
):
    count = star.shape[0] // 2
    parts = (slice(0, count), slice(count, 2 * count))
    loads = [
        pltpu.make_async_copy(extra_hbm, extra, sems.at[0]),
        pltpu.make_async_copy(star_hbm.at[parts[0]], star.at[parts[0]], sems.at[1]),
        pltpu.make_async_copy(star_hbm.at[parts[1]], star.at[parts[1]], sems.at[2]),
        pltpu.make_async_copy(tracer_hbm, tracer, sems.at[3]),
    ]
    for load in loads:
        load.start()
    loads[0].wait()
    stores = [pltpu.make_async_copy(extra.at[3], surface_out, sems.at[4])]
    stores[0].start()
    for comp in range(2):
        loads[1 + comp].wait()

        def correct(level, carry):
            k = comp * count + level
            wet = level.astype(F32) < extra[2]
            corrected[k] = star[k] + jnp.where(wet, extra[comp], 0.0)
            return carry

        lax.fori_loop(0, count, correct, 0)
        store = pltpu.make_async_copy(corrected.at[parts[comp]], velocity_out.at[parts[comp]], sems.at[5 + comp])
        store.start()
        stores.append(store)
    loads[3].wait()
    stores.append(pltpu.make_async_copy(tracer, tracer_out, sems.at[7]))
    stores[-1].start()
    for store in stores:
        store.wait()


def per_device(n_lon, n_lat, tracers, velocity, active_levels, diffusivity, viscosity, ocean_depth, wind_forcing):
    _, count, rows, cols = tracers.shape
    kinds = 4 * count + 3
    packed = -(-2 * kinds // 8) * 8
    message = packed + 2 * DEEP
    tall, deep_rows = rows + 2 * PAD, rows + 2 * DEEP
    padded = deep_rows + 2 * PAD
    strip_rows = 8 * -(-(rows // 8) // (cols // STRIP))
    extra = jax.ShapeDtypeStruct((4, rows, cols), F32)
    block = jax.ShapeDtypeStruct((2 * count, rows, cols), F32)
    flat = jax.ShapeDtypeStruct((rows, cols), F32)
    hbm = pl.BlockSpec(memory_space=pltpu.HBM)
    out = pl.pallas_call(
        functools.partial(kernel, n_lon, n_lat),
        out_shape=(block, block, extra),
        in_specs=[hbm] * 7,
        out_specs=(hbm, hbm, hbm),
        scratch_shapes=[
            pltpu.VMEM(block.shape, F32),
            pltpu.VMEM(block.shape, F32),
            pltpu.VMEM(extra.shape, F32),
            pltpu.VMEM((4 * count, tall, cols), F32),
            pltpu.VMEM((3, tall, cols), F32),
            pltpu.VMEM((rows, cols), jnp.int32),
            pltpu.VMEM((2, rows, cols), F32),
            pltpu.VMEM((2, tall, cols), F32),
            pltpu.VMEM((tall, cols), F32),
            pltpu.VMEM((2, tall, cols), F32),
            pltpu.VMEM((3, 4, tall, cols), F32),
            pltpu.VMEM((4, 2, padded, cols), F32),
            pltpu.VMEM((2, padded, cols), F32),
            pltpu.VMEM((11, 2, deep_rows, cols), F32),
            pltpu.VMEM((2, padded, cols), F32),
            pltpu.VMEM((SOLVE_ITERS + 1, 2, padded, cols), F32),
            pltpu.VMEM((2, message, cols), F32),
            pltpu.VMEM((2, message, cols), F32),
            pltpu.VMEM((2, rows, cols), F32),
            pltpu.VMEM((2, rows, cols), F32),
            pltpu.VMEM((2, 2, 2, strip_rows, cols), F32),
            pltpu.VMEM((2, 2, 2, strip_rows, cols), F32),
            pltpu.VMEM((2, 4, 24, cols), F32),
            pltpu.VMEM((2, 4, 24, cols), F32),
            pltpu.VMEM((2, 2, DEEP, cols), F32),
            pltpu.VMEM((1, 1, cols), F32),
            pltpu.VMEM((n_lon * n_lat, 1, cols), F32),
            pltpu.SemaphoreType.DMA((7,)),
            pltpu.SemaphoreType.DMA((3,)),
            pltpu.SemaphoreType.DMA((5, 2)),
            pltpu.SemaphoreType.DMA((5, 2)),
            pltpu.SemaphoreType.DMA((2, 4)),
            pltpu.SemaphoreType.DMA((2, 4)),
            pltpu.SemaphoreType.DMA((n_lon * n_lat,)),
            pltpu.SemaphoreType.DMA((n_lon * n_lat,)),
        ],
        compiler_params=pltpu.CompilerParams(
            collective_id=0, has_side_effects=True, vmem_limit_bytes=58 * 1024 * 1024
        ),
    )(
        tracers.reshape(2 * count, rows, cols),
        velocity.reshape(2 * count, rows, cols),
        active_levels,
        diffusivity,
        viscosity,
        ocean_depth,
        wind_forcing,
    )
    out = pl.pallas_call(
        finish,
        out_shape=(block, block, flat),
        in_specs=[hbm] * 3,
        out_specs=(hbm, hbm, hbm),
        scratch_shapes=[
            pltpu.VMEM(block.shape, F32),
            pltpu.VMEM(block.shape, F32),
            pltpu.VMEM(extra.shape, F32),
            pltpu.VMEM(block.shape, F32),
            pltpu.SemaphoreType.DMA((8,)),
        ],
        compiler_params=pltpu.CompilerParams(vmem_limit_bytes=58 * 1024 * 1024),
    )(*out)
    return out[0].reshape(tracers.shape), out[1].reshape(velocity.shape), out[2]


def solution(mesh):
    flat = P("lat", "lon")
    deep = P(None, None, "lat", "lon")
    return jax.shard_map(
        functools.partial(per_device, mesh.shape["lon"], mesh.shape["lat"]),
        mesh=mesh,
        in_specs=(deep, deep, flat, flat, flat, flat, P(None, "lat", "lon")),
        out_specs=(deep, deep, flat),
        check_vma=False,
    )
```

```python
import functools
import math

import jax
import jax.numpy as jnp
from jax import lax
from jax.experimental import pallas as pl
from jax.experimental.pallas import tpu as pltpu
from jax.sharding import PartitionSpec as P

SUBCYCLES = 8
SOLVE_ITERS = 4
flow_step = 0.3
slope_step = 0.3
floor_diag = 0.05

PAD = 8
DEEP = 24
STRIP = 32
MESH = pl.DeviceIdType.MESH
F32 = jnp.float32

SHIFTS = (0.0, 5.0, 2.5, 8.0)
SCALE = 5.0


def roll(x, shift, axis):
    return pltpu.roll(x, shift % x.shape[axis], axis)


def lanes(shape):
    return lax.broadcasted_iota(jnp.int32, shape, len(shape) - 1)


def lane_sides(a, b):
    cols = a.shape[-1]
    lane = lanes(a.shape)
    last, first = lane == cols - 1, lane == 0
    a_up, b_up = roll(a, -1, 1), roll(b, -1, 1)
    a_down, b_down = roll(a, 1, 1), roll(b, 1, 1)
    east = (jnp.where(last, b_up, a_up), jnp.where(last, a_up, b_up))
    west = (jnp.where(first, b_down, a_down), jnp.where(first, a_down, b_down))
    return east, west


def mirrored(x):
    return jnp.take_along_axis(x, x.shape[1] - 1 - lanes(x.shape), axis=1)


def upturned(x):
    ids = 7 - lax.broadcasted_iota(jnp.int32, (8, x.shape[1]), 0)
    tiles = [x[at : at + 8] for at in range(0, x.shape[0], 8)]
    return jnp.concatenate([jnp.take_along_axis(tile, ids, axis=0) for tile in tiles[::-1]], axis=0)


def folded(x):
    return upturned(mirrored(x))


def kernel(
    n_lon,
    n_lat,
    tracer_hbm,
    velocity_hbm,
    levels_hbm,
    diff_hbm,
    visc_hbm,
    depth_hbm,
    wind_hbm,
    tracer_hbm_out,
    star_hbm_out,
    extra_hbm_out,
    tracer_out,
    star_out,
    extra_out,
    fields,
    flats,
    levels_in,
    wind,
    near,
    own_pack,
    firsts,
    laps,
    faces,
    deep,
    ocean,
    weights,
    flux,
    basis,
    row_send,
    row_recv,
    col_send,
    col_recv,
    strip_send,
    strip_recv,
    corner_send,
    corner_recv,
    fold_recv,
    part,
    parts,
    load_sems,
    store_sems,
    send_sems,
    recv_sems,
    corner_send_sems,
    corner_recv_sems,
    sum_send,
    sum_recv,
):
    count = tracer_hbm.shape[0] // 2
    rows, cols = levels_hbm.shape
    top_row = PAD + rows
    deep_rows = rows + 2 * DEEP
    start = PAD + DEEP
    stop = start + rows
    end = PAD + deep_rows
    lon = lax.axis_index("lon")
    lat = lax.axis_index("lat")
    right = lax.rem(lon + 1, n_lon)
    left = lax.rem(lon + n_lon - 1, n_lon)
    mirror = n_lon - 1 - lon
    top = lat == n_lat - 1
    bottom = lat == 0
    above = jnp.minimum(lat + 1, n_lat - 1)
    below = jnp.maximum(lat - 1, 0)

    loads = [
        pltpu.make_async_copy(src, dst, load_sems.at[n])
        for n, (src, dst) in enumerate(
            (
                (velocity_hbm, fields.at[0 : 2 * count, PAD:top_row, :]),
                (tracer_hbm, fields.at[2 * count : 4 * count, PAD:top_row, :]),
                (levels_hbm, levels_in),
                (visc_hbm, flats.at[0, PAD:top_row, :]),
                (diff_hbm, flats.at[1, PAD:top_row, :]),
                (depth_hbm, deep.at[0, 0, start:stop, :]),
                (wind_hbm, wind),
            )
        )
    ]
    for load in loads:
        load.start()

    def remote(src, dst, send, recv, device):
        return pltpu.make_async_remote_copy(
            src_ref=src, dst_ref=dst, send_sem=send, recv_sem=recv, device_id=device, device_id_type=MESH
        )

    barrier = pltpu.get_barrier_semaphore()

    def peer(k):
        return {"lat": lax.rem(lat + k // n_lon, n_lat), "lon": lax.rem(lon + k % n_lon, n_lon)}

    for k in range(1, n_lon * n_lat):
        pl.semaphore_signal(barrier, inc=1, device_id=peer(k), device_id_type=MESH)

    kinds = 4 * count + 3
    packed = -(-2 * kinds // 8) * 8
    row_send[:, 2 * kinds : packed, :] = jnp.zeros((2, packed - 2 * kinds, cols), F32)
    deep[2:4] = jnp.zeros((2,) + deep.shape[1:], F32)
    for array in (flux, ocean):
        array[:, 0:PAD, :] = jnp.zeros((2, PAD, cols), F32)
        array[:, end:, :] = jnp.zeros((2, PAD, cols), F32)
    for array in (basis, deep.at[0:2]):
        array[:, :, 0:PAD, :] = jnp.zeros((array.shape[0], 2, PAD, cols), F32)
        array[:, :, end:, :] = jnp.zeros((array.shape[0], 2, PAD, cols), F32)
    basis[0, :, PAD:end, :] = jnp.zeros((2, deep_rows, cols), F32)
    own_pack[0:PAD, :] = jnp.zeros((PAD, cols), F32)
    own_pack[top_row:, :] = jnp.zeros((PAD, cols), F32)
    @pl.when(bottom)
    def _():
        row_recv[1] = jnp.zeros(row_recv.shape[1:], F32)
        corner_recv[:, 2:4] = jnp.zeros((2, 2) + corner_recv.shape[2:], F32)

    for load in loads:
        load.wait()

    levels_float = levels_in[...].astype(F32)
    flats[2, PAD:top_row, :] = levels_float
    deep[1, 0, start:stop, :] = levels_float

    def block_of(k):
        return (fields, k) if k < 4 * count else (flats, k - 4 * count)

    for k in range(kinds):
        ref, index = block_of(k)
        row_send[0, 2 * k : 2 * k + 2, :] = ref[index, top_row - 2 : top_row, :]
        row_send[1, 2 * k : 2 * k + 1, :] = ref[index, PAD + 1 : PAD + 2, :]
        row_send[1, 2 * k + 1 : 2 * k + 2, :] = ref[index, PAD : PAD + 1, :]
    for f in range(2):
        at = packed + f * DEEP
        row_send[0, at : at + DEEP, :] = deep[f, 0, stop - DEEP : stop, :]
        row_send[1, at : at + DEEP, :] = deep[f, 0, start : start + DEEP, :]

    pl.semaphore_wait(barrier, n_lon * n_lat - 1)

    def rows_out(src, dst, stage):
        @pl.when(top)
        def _():
            remote(src(0), dst(0), send_sems.at[stage, 0], recv_sems.at[stage, 0], {"lon": mirror}).start()

        @pl.when(jnp.logical_not(top))
        def _():
            remote(src(0), dst(1), send_sems.at[stage, 0], recv_sems.at[stage, 1], {"lat": above}).start()

        @pl.when(jnp.logical_not(bottom))
        def _():
            remote(src(1), dst(0), send_sems.at[stage, 1], recv_sems.at[stage, 0], {"lat": below}).start()

    def rows_in(src, dst, stage):
        remote(src(0), dst(0), send_sems.at[stage, 0], recv_sems.at[stage, 0], {"lat": above}).wait_recv()

        @pl.when(jnp.logical_not(bottom))
        def _():
            remote(src(1), dst(1), send_sems.at[stage, 1], recv_sems.at[stage, 1], {"lat": below}).wait_recv()

    def rows_sent(src, dst, stage):
        remote(src(0), dst(0), send_sems.at[stage, 0], recv_sems.at[stage, 0], {"lat": above}).wait_send()

        @pl.when(jnp.logical_not(bottom))
        def _():
            remote(src(1), dst(1), send_sems.at[stage, 1], recv_sems.at[stage, 1], {"lat": below}).wait_send()

    def cols_copies(send, recv, stage):
        return (
            remote(send.at[0], recv.at[0], send_sems.at[stage, 0], recv_sems.at[stage, 0], {"lon": right}),
            remote(send.at[1], recv.at[1], send_sems.at[stage, 1], recv_sems.at[stage, 1], {"lon": left}),
        )

    row_src = lambda i: row_send.at[i]
    row_dst = lambda i: row_recv.at[i]
    rows_out(row_src, row_dst, 0)

    odd_tile = jnp.bitwise_and(lanes((8, cols)), 1) == 1
    pair_of = jnp.right_shift(lanes((8, cols)), 1)
    for at in range(0, rows, 8):
        own = jnp.zeros((8, cols), F32)
        inner = jnp.zeros((8, cols), F32)
        for k in range(kinds):
            ref, index = block_of(k)
            x = ref[index, PAD + at : PAD + at + 8, :]
            pair = pair_of == k
            own = jnp.where(pair, roll(x, 2 * k + 1, 1), own)
            if k < 2 * count or k == kinds - 1:
                inner = jnp.where(pair, jnp.where(odd_tile, roll(x, 2 * k, 1), roll(x, 2 * k + 2, 1)), inner)
        own_pack[PAD + at : PAD + at + 8, :] = own
        col_send[1, at : at + 8, :] = jnp.where(odd_tile, own, roll(inner, -1, 1))
        col_send[0, at : at + 8, :] = jnp.where(odd_tile, roll(inner, 1, 1), own)
    col_copies = cols_copies(col_send, col_recv, 1)
    for copy in col_copies:
        copy.start()

    groups = cols // STRIP
    tiles = rows // 8
    rim_tiles = DEEP // 8
    group_of = lanes((8, cols)) // STRIP

    def strip_of(ref, base, first_row, number):
        strip = None
        for g in range(number):
            at = first_row + 8 * g
            x = roll(ref[at : at + 8, :], STRIP * g - base, 1)
            strip = x if strip is None else jnp.where(group_of == g, x, strip)
        return strip

    def pack_strips(pair, f):
        ref = deep.at[2 * pair + f, 0]
        for side, base in ((0, cols - STRIP), (1, 0)):
            for t in range(0, tiles, groups):
                at = 8 * (t // groups)
                strip_send[pair, side, f, at : at + 8, :] = strip_of(
                    ref, base, start + 8 * t, min(groups, tiles - t)
                )
            for corner, first_row in ((side, stop - DEEP), (2 + side, start)):
                corner_send[pair, corner, 8 * f : 8 * f + 8, :] = strip_of(ref, base, first_row, rim_tiles)

    def fill(pair, f, at, west_tile, east_tile, g):
        low = roll(east_tile, -STRIP * g, 1)
        high = roll(west_tile, cols - STRIP - STRIP * g, 1)
        deep[2 * pair + f, 1, at : at + 8, :] = jnp.where(group_of < groups // 2, low, high)

    def unpack_strips(pair, f, sign):
        for j in range(tiles):
            at = 8 * (j // groups)
            west_tile = strip_recv[pair, 0, f, at : at + 8, :]
            east_tile = strip_recv[pair, 1, f, at : at + 8, :]
            fill(pair, f, start + 8 * j, west_tile, east_tile, j % groups)
        tile_at = slice(8 * f, 8 * f + 8)

        @pl.when(top)
        def _():
            for corner in range(2):
                tile = folded(corner_recv[pair, corner, tile_at, :])
                corner_recv[pair, corner, tile_at, :] = sign * roll(tile, -STRIP, 1)

        for j in range(rim_tiles):
            fill(pair, f, stop + 8 * j, corner_recv[pair, 1, tile_at, :], corner_recv[pair, 0, tile_at, :], j)
            fill(
                pair, f, PAD + 8 * j, corner_recv[pair, 3, tile_at, :], corner_recv[pair, 2, tile_at, :], j
            )

    turned_lon = (lax.rem(2 * n_lon - 2 - lon, n_lon), lax.rem(n_lon - lon, n_lon))
    alone = [jnp.logical_and(top, turned == lon) for turned in turned_lon]

    def corner_copy(pair, corner, slot, device):
        size = 24 if pair == 0 else 16
        return remote(
            corner_send.at[pair, corner, 0:size, :],
            corner_recv.at[pair, slot, 0:size, :],
            corner_send_sems.at[pair, corner],
            corner_recv_sems.at[pair, slot],
            device,
        )

    def corners_out(pair):
        for corner in range(2):
            side = right if corner == 0 else left

            @pl.when(jnp.logical_not(top))
            def _():
                corner_copy(pair, corner, 3 - corner, {"lat": above, "lon": side}).start()

            @pl.when(jnp.logical_and(top, turned_lon[corner] != lon))
            def _():
                corner_copy(pair, corner, corner, {"lon": turned_lon[corner]}).start()

            @pl.when(alone[corner])
            def _():
                corner_recv[pair, corner] = corner_send[pair, corner]

            @pl.when(jnp.logical_not(bottom))
            def _():
                corner_copy(pair, 2 + corner, 1 - corner, {"lat": below, "lon": side}).start()

    def corners_each(pair, act):
        for corner in range(2):
            side = right if corner == 0 else left

            @pl.when(jnp.logical_not(alone[corner]))
            def _():
                act(corner_copy(pair, corner, corner, {"lat": above, "lon": side}))

            @pl.when(jnp.logical_not(bottom))
            def _():
                act(corner_copy(pair, 2 + corner, 2 + corner, {"lat": below, "lon": side}))

    for corner in range(4):
        at = rows - 8 if corner < 2 else 0
        corner_send[0, corner, 16:24, :] = own_pack[PAD + at : PAD + at + 8, :]
    for f in range(2):
        pack_strips(0, f)
    corners_out(0)
    stat_copies = cols_copies(strip_send.at[0], strip_recv.at[0], 2)
    for copy in stat_copies:
        copy.start()

    row_ids = (lat * rows + lax.broadcasted_iota(jnp.int32, (rows, cols), 0)).astype(F32)
    coriolis = 0.25 * jnp.sin(math.pi * ((row_ids + 0.5) / (rows * n_lat) - 0.5))
    faces[2, 2, 0:rows, :] = coriolis

    rows_in(row_src, row_dst, 0)

    @pl.when(top)
    def _():
        turned = mirrored(row_recv[0])
        ids = lax.broadcasted_iota(jnp.int32, turned.shape, 0)
        turned = jnp.where(ids < 4 * count, -turned, turned)
        row_recv[0, 0:packed, :] = turned[0:packed]
        for f in range(2):
            at = packed + f * DEEP
            row_recv[0, at : at + DEEP, :] = upturned(turned[at : at + DEEP])

    for f in range(2):
        at = packed + f * DEEP
        deep[f, 0, PAD:start, :] = row_recv[1, at : at + DEEP, :]
        deep[f, 0, stop:end, :] = row_recv[0, at : at + DEEP, :]

    for k in range(kinds):
        ref, index = block_of(k)
        ref[index, top_row : top_row + 1, :] = row_recv[0, 2 * k + 1 : 2 * k + 2, :]
        ref[index, top_row + 1 : top_row + 2, :] = row_recv[0, 2 * k : 2 * k + 1, :]
        ref[index, PAD - 2 : PAD, :] = row_recv[1, 2 * k : 2 * k + 2, :]

    for copy in col_copies:
        copy.wait_recv()
    corners_each(0, lambda copy: copy.wait_recv())
    tall = rows + 2 * PAD
    lane = lanes((tall, cols))
    odd = jnp.bitwise_and(lane, 1) == 1
    from_west, from_east = col_recv[0], col_recv[1]
    near[1] = jnp.zeros((tall, cols), F32)
    near[0] = jnp.zeros((tall, cols), F32)
    odd_here = odd[0:rows]
    near[1, PAD:top_row, :] = jnp.where(odd_here, roll(from_west, 1, 1), roll(from_east, -1, 1))
    near[0, PAD:top_row, :] = jnp.where(odd_here, from_west, from_east)
    ne, nw, se, sw = [corner_recv[0, corner, 16:24, :] for corner in range(4)]
    below_tile = jnp.where(odd_tile, roll(sw, 1, 1), roll(se, -1, 1))
    near[1, PAD - 1 : PAD, :] = below_tile[7:8]

    @pl.when(top)
    def _():
        tile = jnp.where(odd_tile, nw, ne)
        tile = jnp.where(lanes((8, cols)) < 4 * count, -tile, tile)
        near[1, top_row : top_row + 1, :] = tile[7:8]

    @pl.when(jnp.logical_not(top))
    def _():
        tile = jnp.where(odd_tile, roll(nw, 1, 1), roll(ne, -1, 1))
        near[1, top_row : top_row + 1, :] = tile[0:1]

    close, far = near[1], near[0]
    own = own_pack[...]

    level_of = lax.rem(jnp.right_shift(lane, 1), count).astype(F32)

    def packed_wet(pack):
        at = 2 * (kinds - 1)
        level = jnp.where(odd, pack[:, at + 1 : at + 2], pack[:, at : at + 1])
        return jnp.where(level_of < level, 1.0, 0.0)

    wet_own, wet_close, wet_far = packed_wet(own), packed_wet(close), packed_wet(far)
    firsts[...] = wet_close * (
        wet_own * (own - close)
        + wet_far * (far - close)
        + roll(wet_close, -1, 0) * (roll(close, -1, 0) - close)
        + roll(wet_close, 1, 0) * (roll(close, 1, 0) - close)
    )

    def sides(x, pack, k):
        rim = pltpu.roll(pack, cols - 1 - 2 * k, 1)
        lane = lanes(x.shape)
        return (
            jnp.where(lane == cols - 1, rim, roll(x, -1, 1)),
            jnp.where(lane == 0, rim, roll(x, 1, 1)),
        )

    whole = slice(PAD, top_row)
    northern = slice(PAD + 1, top_row + 1)
    southern = slice(PAD - 1, top_row - 1)
    for index in range(2):
        c = flats[index, whole, :]
        c_east, c_west = sides(c, near[1, whole, :], 4 * count + index)
        others = (c_east, c_west, flats[index, northern, :], flats[index, southern, :])
        for n, other in enumerate(others):
            faces[index, n, 0:rows, :] = 0.5 * (c + other)
    lev_east, lev_west = sides(flats[2], near[1], kinds - 1)
    faces[2, 0] = lev_east
    faces[2, 1] = lev_west

    def masks(level, here):
        return (
            level < flats[2, here : here + 8, :],
            level < faces[2, 0, here : here + 8, :],
            level < faces[2, 1, here : here + 8, :],
            level < flats[2, here + 1 : here + 9, :],
            level < flats[2, here - 1 : here + 7, :],
        )

    def weighted(x, neighbours, wets, index, at):
        total = None
        for n, other in enumerate(neighbours):
            term = faces[index, n, at : at + 8, :] * jnp.where(wets[n + 1], other - x, 0.0)
            total = term if total is None else total + term
        return total

    def velocity_level(level, carry):
        level_float = level.astype(F32)
        for at in range(0, rows + 8, 8):
            here = PAD - 1 + at
            wets = masks(level_float, here)
            for comp in range(2):
                k = comp * count + level
                x = fields[k, here : here + 8, :]
                x_east, x_west = sides(x, near[1, here : here + 8, :], k)
                first = (
                    jnp.where(wets[1], x_east - x, 0.0)
                    + jnp.where(wets[2], x_west - x, 0.0)
                    + jnp.where(wets[3], fields[k, here + 1 : here + 9, :] - x, 0.0)
                    + jnp.where(wets[4], fields[k, here - 1 : here + 7, :] - x, 0.0)
                )
                laps[comp, at : at + 8, :] = jnp.where(wets[0], first, 0.0)
        for at in range(0, rows, 8):
            here = PAD + at
            wets = masks(level_float, here)
            for comp in range(2):
                k = comp * count + level
                x = laps[comp, at + 1 : at + 9, :]
                x_east, x_west = sides(x, firsts[here : here + 8, :], k)
                others = (x_east, x_west, laps[comp, at + 2 : at + 10, :], laps[comp, at : at + 8, :])
                second = weighted(x, others, wets, 0, at)
                other = fields[(1 - comp) * count + level, here : here + 8, :]
                turned = faces[2, 2, at : at + 8, :] * other
                star = fields[k, here : here + 8, :] - second
                star = jnp.where(wets[0], star + turned if comp == 0 else star - turned, 0.0)
                star_out[k, at : at + 8, :] = star
                deep[2 + comp, 0, start + at : start + at + 8, :] += star
        return carry

    lax.fori_loop(0, count, velocity_level, 0)

    levels_here = flats[2, whole, :]
    ocean_here = jnp.where(levels_here > 0, 1.0, 0.0)
    for comp in range(2):
        mean = deep[2 + comp, 0, start:stop, :] / jnp.maximum(levels_here, 1.0)
        extra_out[comp] = mean
        deep[2 + comp, 0, start:stop, :] = mean + wind[comp] * ocean_here

    def flow_edge(i):
        at = stop - DEEP if i == 0 else start
        return deep.at[2:4, 0, at : at + DEEP, :]

    fold_dst = lambda i: fold_recv.at[i]
    rows_out(flow_edge, fold_dst, 3)
    for comp in range(2):
        pack_strips(1, comp)
    flow_copies = cols_copies(strip_send.at[1], strip_recv.at[1], 4)
    for copy in flow_copies:
        copy.start()
    corners_out(1)
    stores = [pltpu.make_async_copy(star_out, star_hbm_out, store_sems.at[0])]
    stores[0].start()

    def tracer_level(level, carry):
        for at in range(0, rows, 8):
            here = PAD + at
            wets = masks(level.astype(F32), here)
            for comp in range(2):
                k = 2 * count + comp * count + level
                x = fields[k, here : here + 8, :]
                x_east, x_west = sides(x, near[1, here : here + 8, :], k)
                others = (x_east, x_west, fields[k, here + 1 : here + 9, :], fields[k, here - 1 : here + 7, :])
                change = weighted(x, others, wets, 1, at)
                tracer_out[comp * count + level, at : at + 8, :] = x + jnp.where(wets[0], change, 0.0)
        return carry

    lax.fori_loop(0, count, tracer_level, 0)
    stores.append(pltpu.make_async_copy(tracer_out, tracer_hbm_out, store_sems.at[1]))
    stores[1].start()

    for copy in stat_copies:
        copy.wait_recv()
    for f in range(2):
        unpack_strips(0, f, 1.0)
    both = range(2)

    def around(ref, at):
        result = []
        for shift in (0, 1, -1):
            p = [ref[n, at + shift : at + shift + 8, :] for n in both]
            result += list(lane_sides(*p)) + ([] if shift == 0 else [p])
        return result

    scales = (1.0, 1.0, 0.5, 0.5, 1.0, 0.5, 0.5, 1.0)
    for tile in both:
        ocean[tile, PAD:end, :] = jnp.where(deep[1, tile, PAD:end, :] > 0, 1.0, 0.0)
    for at in range(0, deep_rows, 8):
        depth_here = [deep[0, n, PAD + at : PAD + at + 8, :] for n in both]
        wet_here = [ocean[n, PAD + at : PAD + at + 8, :] for n in both]
        totals = [floor_diag * wet_here[n] + (1.0 - wet_here[n]) for n in both]
        sums = zip(scales, around(deep.at[0], PAD + at), around(ocean, PAD + at))
        for index, (scale, d, o) in enumerate(sums):
            for n in both:
                weight = scale * 0.5 * (depth_here[n] + d[n]) * wet_here[n] * o[n]
                weights[index, n, at : at + 8, :] = weight
                totals[n] = totals[n] + weight
        for n in both:
            weights[8, n, at : at + 8, :] = totals[n]
            weights[9, n, at : at + 8, :] = 0.5 * flow_step * wet_here[n]
            weights[10, n, at : at + 8, :] = 0.5 * slope_step * wet_here[n]

    for copy in flow_copies:
        copy.wait_recv()
    corners_each(1, lambda copy: copy.wait_recv())
    rows_in(flow_edge, fold_dst, 3)
    for comp in range(2):
        unpack_strips(1, comp, -1.0)

    @pl.when(top)
    def _():
        for comp in range(2):
            fold_recv[0, comp] = -folded(fold_recv[0, comp])

    for comp in range(2):
        deep[2 + comp, 0, stop:end, :] = fold_recv[0, comp]

    @pl.when(jnp.logical_not(bottom))
    def _():
        for comp in range(2):
            deep[2 + comp, 0, PAD:start, :] = fold_recv[1, comp]

    rows_sent(flow_edge, fold_dst, 3)

    def subcycle(step, carry):
        for at in range(0, deep_rows, 8):
            here = slice(PAD + at, PAD + at + 8)
            up = slice(PAD + at + 1, PAD + at + 9)
            down = slice(PAD + at - 1, PAD + at + 7)
            easts, wests = lane_sides(*[deep[0, n, here, :] * deep[2, n, here, :] for n in both])
            for n in both:
                divergence = (easts[n] - wests[n]) + (
                    deep[0, n, up, :] * deep[3, n, up, :] - deep[0, n, down, :] * deep[3, n, down, :]
                )
                basis[0, n, here, :] = basis[0, n, here, :] - weights[9, n, at : at + 8, :] * divergence
        for at in range(0, deep_rows, 8):
            here = slice(PAD + at, PAD + at + 8)
            easts, wests = lane_sides(*[basis[0, n, here, :] for n in both])
            for n in both:
                slope = weights[10, n, at : at + 8, :]
                deep[2, n, here, :] = deep[2, n, here, :] - slope * (easts[n] - wests[n])
                deep[3, n, here, :] = deep[3, n, here, :] - slope * (
                    basis[0, n, PAD + at + 1 : PAD + at + 9, :] - basis[0, n, PAD + at - 1 : PAD + at + 7, :]
                )
        return carry

    lax.fori_loop(0, SUBCYCLES, subcycle, 0)

    for k in range(SOLVE_ITERS):
        for at in range(0, deep_rows, 8):
            here = slice(PAD + at, PAD + at + 8)
            summed = [(weights[8, n, at : at + 8, :] - SHIFTS[k]) * basis[k, n, here, :] for n in both]
            for index, term in enumerate(around(basis.at[k], PAD + at)):
                for n in both:
                    summed[n] = summed[n] - weights[index, n, at : at + 8, :] * term[n]
            for n in both:
                basis[k + 1, n, here, :] = summed[n] * (1.0 / SCALE)

    pairs = [(i, j) for i in range(SOLVE_ITERS) for j in range(i, SOLVE_ITERS + 1)]
    products = [None] * len(pairs)
    for at in range(start, stop, 8):
        inside = [basis[k, 0, at : at + 8, :] for k in range(SOLVE_ITERS + 1)]
        for n, (i, j) in enumerate(pairs):
            term = inside[i] * inside[j]
            products[n] = term if products[n] is None else products[n] + term
    lane_row = lanes((1, cols))
    packed_sums = jnp.zeros((1, cols), F32)
    for n, (i, j) in enumerate(pairs):
        value = jnp.sum(jnp.sum(products[n], axis=0, keepdims=True), axis=1, keepdims=True)
        packed_sums = jnp.where(lane_row == n, value, packed_sums)
    me = lat * n_lon + lon
    part[0] = packed_sums
    parts[me] = packed_sums

    def sum_copy(k):
        return remote(part, parts.at[pl.ds(me, 1)], sum_send.at[k], sum_recv.at[k], peer(k))

    sum_copies = [sum_copy(k) for k in range(1, n_lon * n_lat)]
    for copy in sum_copies:
        copy.start()
    for copy in sum_copies:
        copy.wait()
    sums = parts[0]
    for n in range(1, n_lon * n_lat):
        sums = sums + parts[n]
    sums = jnp.broadcast_to(sums, (8, cols))
    gram = {}
    for n, (i, j) in enumerate(pairs):
        gram[i, j] = gram[j, i] = jnp.broadcast_to(sums[:, n : n + 1], (8, cols))

    def inner_product(a, b):
        result = None
        for i, x in a.items():
            for j, y in b.items():
                term = x * y * gram[i, j]
                result = term if result is None else result + term
        return result

    def image_of(a):
        result = {}
        for n, x in a.items():
            for at, value in ((n, SHIFTS[n] * x), (n + 1, SCALE * x)):
                result[at] = result[at] + value if at in result else value
        return result

    one = jnp.ones((8, cols), F32)
    residual = {0: one}
    direction = {0: one}
    answer = {}
    norm = gram[0, 0]
    for iteration in range(SOLVE_ITERS):
        image = image_of(direction)
        step = norm / inner_product(direction, image)
        for n, x in direction.items():
            answer[n] = answer[n] + step * x if n in answer else step * x
        if iteration < SOLVE_ITERS - 1:
            residual = {n: (residual[n] if n in residual else 0.0) - step * x for n, x in image.items()}
            new_norm = inner_product(residual, residual)
            ratio = new_norm / norm
            direction = {
                n: x + ratio * direction[n] if n in direction else x for n, x in residual.items()
            }
            norm = new_norm
    for at in range(start - 8, stop + 8, 8):
        for tile in both:
            surface = None
            for n, x in answer.items():
                term = x * basis[n, tile, at : at + 8, :]
                surface = term if surface is None else surface + term
            flux[tile, at : at + 8, :] = surface

    easts, wests = lane_sides(flux[0, start:stop, :], flux[1, start:stop, :])
    slopes = (easts[0] - wests[0], flux[0, start + 1 : stop + 1, :] - flux[0, start - 1 : stop - 1, :])
    for comp, slope in enumerate(slopes):
        final = deep[2 + comp, 0, start:stop, :] - weights[10, 0, DEEP : DEEP + rows, :] * slope
        extra_out[comp] = final - extra_out[comp]
    extra_out[2] = levels_here
    extra_out[3] = flux[0, start:stop, :]
    stores.append(pltpu.make_async_copy(extra_out, extra_hbm_out, store_sems.at[2]))
    stores[2].start()
    rows_sent(row_src, row_dst, 0)
    for pair in range(2):
        corners_each(pair, lambda copy: copy.wait_send())
    for copy in col_copies + stat_copies + flow_copies:
        copy.wait_send()
    for store in stores:
        store.wait()


def finish(
    tracer_hbm, star_hbm, extra_hbm, tracer_out, velocity_out, surface_out, tracer, star, extra, corrected, sems
):
    count = star.shape[0] // 2
    parts = (slice(0, count), slice(count, 2 * count))
    loads = [
        pltpu.make_async_copy(extra_hbm, extra, sems.at[0]),
        pltpu.make_async_copy(star_hbm.at[parts[0]], star.at[parts[0]], sems.at[1]),
        pltpu.make_async_copy(star_hbm.at[parts[1]], star.at[parts[1]], sems.at[2]),
        pltpu.make_async_copy(tracer_hbm, tracer, sems.at[3]),
    ]
    for load in loads:
        load.start()
    loads[0].wait()
    stores = [pltpu.make_async_copy(extra.at[3], surface_out, sems.at[4])]
    stores[0].start()
    for comp in range(2):
        loads[1 + comp].wait()

        def correct(level, carry):
            k = comp * count + level
            wet = level.astype(F32) < extra[2]
            corrected[k] = star[k] + jnp.where(wet, extra[comp], 0.0)
            return carry

        lax.fori_loop(0, count, correct, 0)
        store = pltpu.make_async_copy(corrected.at[parts[comp]], velocity_out.at[parts[comp]], sems.at[5 + comp])
        store.start()
        stores.append(store)
    loads[3].wait()
    stores.append(pltpu.make_async_copy(tracer, tracer_out, sems.at[7]))
    stores[-1].start()
    for store in stores:
        store.wait()


def per_device(n_lon, n_lat, tracers, velocity, active_levels, diffusivity, viscosity, ocean_depth, wind_forcing):
    _, count, rows, cols = tracers.shape
    kinds = 4 * count + 3
    packed = -(-2 * kinds // 8) * 8
    message = packed + 2 * DEEP
    tall, deep_rows = rows + 2 * PAD, rows + 2 * DEEP
    padded = deep_rows + 2 * PAD
    strip_rows = 8 * -(-(rows // 8) // (cols // STRIP))
    extra = jax.ShapeDtypeStruct((4, rows, cols), F32)
    block = jax.ShapeDtypeStruct((2 * count, rows, cols), F32)
    flat = jax.ShapeDtypeStruct((rows, cols), F32)
    hbm = pl.BlockSpec(memory_space=pltpu.HBM)
    out = pl.pallas_call(
        functools.partial(kernel, n_lon, n_lat),
        out_shape=(block, block, extra),
        in_specs=[hbm] * 7,
        out_specs=(hbm, hbm, hbm),
        scratch_shapes=[
            pltpu.VMEM(block.shape, F32),
            pltpu.VMEM(block.shape, F32),
            pltpu.VMEM(extra.shape, F32),
            pltpu.VMEM((4 * count, tall, cols), F32),
            pltpu.VMEM((3, tall, cols), F32),
            pltpu.VMEM((rows, cols), jnp.int32),
            pltpu.VMEM((2, rows, cols), F32),
            pltpu.VMEM((2, tall, cols), F32),
            pltpu.VMEM((tall, cols), F32),
            pltpu.VMEM((tall, cols), F32),
            pltpu.VMEM((2, tall, cols), F32),
            pltpu.VMEM((3, 4, tall, cols), F32),
            pltpu.VMEM((4, 2, padded, cols), F32),
            pltpu.VMEM((2, padded, cols), F32),
            pltpu.VMEM((11, 2, deep_rows, cols), F32),
            pltpu.VMEM((2, padded, cols), F32),
            pltpu.VMEM((SOLVE_ITERS + 1, 2, padded, cols), F32),
            pltpu.VMEM((2, message, cols), F32),
            pltpu.VMEM((2, message, cols), F32),
            pltpu.VMEM((2, rows, cols), F32),
            pltpu.VMEM((2, rows, cols), F32),
            pltpu.VMEM((2, 2, 2, strip_rows, cols), F32),
            pltpu.VMEM((2, 2, 2, strip_rows, cols), F32),
            pltpu.VMEM((2, 4, 24, cols), F32),
            pltpu.VMEM((2, 4, 24, cols), F32),
            pltpu.VMEM((2, 2, DEEP, cols), F32),
            pltpu.VMEM((1, 1, cols), F32),
            pltpu.VMEM((n_lon * n_lat, 1, cols), F32),
            pltpu.SemaphoreType.DMA((7,)),
            pltpu.SemaphoreType.DMA((3,)),
            pltpu.SemaphoreType.DMA((5, 2)),
            pltpu.SemaphoreType.DMA((5, 2)),
            pltpu.SemaphoreType.DMA((2, 4)),
            pltpu.SemaphoreType.DMA((2, 4)),
            pltpu.SemaphoreType.DMA((n_lon * n_lat,)),
            pltpu.SemaphoreType.DMA((n_lon * n_lat,)),
        ],
        compiler_params=pltpu.CompilerParams(
            collective_id=0, has_side_effects=True, vmem_limit_bytes=58 * 1024 * 1024
        ),
    )(
        tracers.reshape(2 * count, rows, cols),
        velocity.reshape(2 * count, rows, cols),
        active_levels,
        diffusivity,
        viscosity,
        ocean_depth,
        wind_forcing,
    )
    out = pl.pallas_call(
        finish,
        out_shape=(block, block, flat),
        in_specs=[hbm] * 3,
        out_specs=(hbm, hbm, hbm),
        scratch_shapes=[
            pltpu.VMEM(block.shape, F32),
            pltpu.VMEM(block.shape, F32),
            pltpu.VMEM(extra.shape, F32),
            pltpu.VMEM(block.shape, F32),
            pltpu.SemaphoreType.DMA((8,)),
        ],
        compiler_params=pltpu.CompilerParams(vmem_limit_bytes=58 * 1024 * 1024),
    )(*out)
    return out[0].reshape(tracers.shape), out[1].reshape(velocity.shape), out[2]


def solution(mesh):
    flat = P("lat", "lon")
    deep = P(None, None, "lat", "lon")
    return jax.shard_map(
        functools.partial(per_device, mesh.shape["lon"], mesh.shape["lat"]),
        mesh=mesh,
        in_specs=(deep, deep, flat, flat, flat, flat, P(None, "lat", "lon")),
        out_specs=(deep, deep, flat),
        check_vma=False,
    )
```

```python
import functools
import math

import jax
import jax.numpy as jnp
from jax import lax
from jax.experimental import pallas as pl
from jax.experimental.pallas import tpu as pltpu
from jax.sharding import PartitionSpec as P

SUBCYCLES = 8
SOLVE_ITERS = 4
flow_step = 0.3
slope_step = 0.3
floor_diag = 0.05

PAD = 8
DEEP = 24
STRIP = 32
MESH = pl.DeviceIdType.MESH
F32 = jnp.float32

SHIFTS = (0.0, 5.0, 2.5, 8.0)
SCALE = 5.0


def roll(x, shift, axis):
    return pltpu.roll(x, shift % x.shape[axis], axis)


def lanes(shape):
    return lax.broadcasted_iota(jnp.int32, shape, len(shape) - 1)


def lane_sides(a, b):
    cols = a.shape[-1]
    lane = lanes(a.shape)
    last, first = lane == cols - 1, lane == 0
    a_up, b_up = roll(a, -1, 1), roll(b, -1, 1)
    a_down, b_down = roll(a, 1, 1), roll(b, 1, 1)
    east = (jnp.where(last, b_up, a_up), jnp.where(last, a_up, b_up))
    west = (jnp.where(first, b_down, a_down), jnp.where(first, a_down, b_down))
    return east, west


def mirrored(x):
    return jnp.take_along_axis(x, x.shape[1] - 1 - lanes(x.shape), axis=1)


def upturned(x):
    ids = 7 - lax.broadcasted_iota(jnp.int32, (8, x.shape[1]), 0)
    tiles = [x[at : at + 8] for at in range(0, x.shape[0], 8)]
    return jnp.concatenate([jnp.take_along_axis(tile, ids, axis=0) for tile in tiles[::-1]], axis=0)


def folded(x):
    return upturned(mirrored(x))


def kernel(
    n_lon,
    n_lat,
    tracer_hbm,
    velocity_hbm,
    levels_hbm,
    diff_hbm,
    visc_hbm,
    depth_hbm,
    wind_hbm,
    tracer_hbm_out,
    star_hbm_out,
    extra_hbm_out,
    tracer_out,
    star_out,
    extra_out,
    fields,
    flats,
    levels_in,
    wind,
    near,
    own_pack,
    firsts,
    laps,
    faces,
    deep,
    ocean,
    weights,
    flux,
    basis,
    row_send,
    row_recv,
    col_send,
    col_recv,
    strip_send,
    strip_recv,
    corner_send,
    corner_recv,
    fold_recv,
    part,
    parts,
    load_sems,
    store_sems,
    send_sems,
    recv_sems,
    corner_send_sems,
    corner_recv_sems,
    sum_send,
    sum_recv,
):
    count = tracer_hbm.shape[0] // 2
    rows, cols = levels_hbm.shape
    top_row = PAD + rows
    deep_rows = rows + 2 * DEEP
    start = PAD + DEEP
    stop = start + rows
    end = PAD + deep_rows
    lon = lax.axis_index("lon")
    lat = lax.axis_index("lat")
    right = lax.rem(lon + 1, n_lon)
    left = lax.rem(lon + n_lon - 1, n_lon)
    mirror = n_lon - 1 - lon
    top = lat == n_lat - 1
    bottom = lat == 0
    above = jnp.minimum(lat + 1, n_lat - 1)
    below = jnp.maximum(lat - 1, 0)

    loads = [
        pltpu.make_async_copy(src, dst, load_sems.at[n])
        for n, (src, dst) in enumerate(
            (
                (velocity_hbm, fields.at[0 : 2 * count, PAD:top_row, :]),
                (tracer_hbm, fields.at[2 * count : 4 * count, PAD:top_row, :]),
                (levels_hbm, levels_in),
                (visc_hbm, flats.at[0, PAD:top_row, :]),
                (diff_hbm, flats.at[1, PAD:top_row, :]),
                (depth_hbm, deep.at[0, 0, start:stop, :]),
                (wind_hbm, wind),
            )
        )
    ]
    for load in loads:
        load.start()

    def remote(src, dst, send, recv, device):
        return pltpu.make_async_remote_copy(
            src_ref=src, dst_ref=dst, send_sem=send, recv_sem=recv, device_id=device, device_id_type=MESH
        )

    barrier = pltpu.get_barrier_semaphore()

    def peer(k):
        return {"lat": lax.rem(lat + k // n_lon, n_lat), "lon": lax.rem(lon + k % n_lon, n_lon)}

    for k in range(1, n_lon * n_lat):
        pl.semaphore_signal(barrier, inc=1, device_id=peer(k), device_id_type=MESH)

    kinds = 4 * count + 3
    deep[2:4] = jnp.zeros((2,) + deep.shape[1:], F32)
    for array in (flux, ocean):
        array[:, 0:PAD, :] = jnp.zeros((2, PAD, cols), F32)
        array[:, end:, :] = jnp.zeros((2, PAD, cols), F32)
    for array in (basis, deep.at[0:2]):
        array[:, :, 0:PAD, :] = jnp.zeros((array.shape[0], 2, PAD, cols), F32)
        array[:, :, end:, :] = jnp.zeros((array.shape[0], 2, PAD, cols), F32)
    basis[0, :, PAD:end, :] = jnp.zeros((2, deep_rows, cols), F32)
    own_pack[0:PAD, :] = jnp.zeros((PAD, cols), F32)
    own_pack[top_row:, :] = jnp.zeros((PAD, cols), F32)
    @pl.when(bottom)
    def _():
        row_recv[1] = jnp.zeros(row_recv.shape[1:], F32)
        deep[0:2, 0, PAD:start, :] = jnp.zeros((2, DEEP, cols), F32)
        corner_recv[:, 2:4] = jnp.zeros((2, 2) + corner_recv.shape[2:], F32)

    for load in loads:
        load.wait()

    levels_float = levels_in[...].astype(F32)
    flats[2, PAD:top_row, :] = levels_float
    deep[1, 0, start:stop, :] = levels_float

    def block_of(k):
        return (fields, k) if k < 4 * count else (flats, k - 4 * count)

    def row_of(k):
        if k < 2 * count:
            return 2 * k + 1, True
        if k == kinds - 1:
            return 4 * count + 1, True
        return 2 * count + 2 + k, False

    for k in range(kinds):
        ref, index = block_of(k)
        at, both_rows = row_of(k)
        row_send[0, at : at + 1, :] = ref[index, top_row - 1 : top_row, :]
        row_send[1, at : at + 1, :] = ref[index, PAD : PAD + 1, :]
        if both_rows:
            row_send[0, at - 1 : at, :] = ref[index, top_row - 2 : top_row - 1, :]
            row_send[1, at - 1 : at, :] = ref[index, PAD + 1 : PAD + 2, :]

    pl.semaphore_wait(barrier, n_lon * n_lat - 1)

    def rows_out(src, dst, stage):
        @pl.when(top)
        def _():
            remote(src(0), dst(0), send_sems.at[stage, 0], recv_sems.at[stage, 0], {"lon": mirror}).start()

        @pl.when(jnp.logical_not(top))
        def _():
            remote(src(0), dst(1), send_sems.at[stage, 0], recv_sems.at[stage, 1], {"lat": above}).start()

        @pl.when(jnp.logical_not(bottom))
        def _():
            remote(src(1), dst(0), send_sems.at[stage, 1], recv_sems.at[stage, 0], {"lat": below}).start()

    def rows_in(src, dst, stage):
        remote(src(0), dst(0), send_sems.at[stage, 0], recv_sems.at[stage, 0], {"lat": above}).wait_recv()

        @pl.when(jnp.logical_not(bottom))
        def _():
            remote(src(1), dst(1), send_sems.at[stage, 1], recv_sems.at[stage, 1], {"lat": below}).wait_recv()

    def rows_sent(src, dst, stage):
        remote(src(0), dst(0), send_sems.at[stage, 0], recv_sems.at[stage, 0], {"lat": above}).wait_send()

        @pl.when(jnp.logical_not(bottom))
        def _():
            remote(src(1), dst(1), send_sems.at[stage, 1], recv_sems.at[stage, 1], {"lat": below}).wait_send()

    def cols_copies(send, recv, stage):
        return (
            remote(send.at[0], recv.at[0], send_sems.at[stage, 0], recv_sems.at[stage, 0], {"lon": right}),
            remote(send.at[1], recv.at[1], send_sems.at[stage, 1], recv_sems.at[stage, 1], {"lon": left}),
        )

    row_src = lambda i: row_send.at[i]
    row_dst = lambda i: row_recv.at[i]
    rows_out(row_src, row_dst, 0)

    odd_tile = jnp.bitwise_and(lanes((8, cols)), 1) == 1
    pair_of = jnp.right_shift(lanes((8, cols)), 1)
    for at in range(0, rows, 8):
        own = jnp.zeros((8, cols), F32)
        inner = jnp.zeros((8, cols), F32)
        for k in range(kinds):
            ref, index = block_of(k)
            x = ref[index, PAD + at : PAD + at + 8, :]
            pair = pair_of == k
            own = jnp.where(pair, roll(x, 2 * k + 1, 1), own)
            if k < 2 * count or k == kinds - 1:
                inner = jnp.where(pair, jnp.where(odd_tile, roll(x, 2 * k, 1), roll(x, 2 * k + 2, 1)), inner)
        own_pack[PAD + at : PAD + at + 8, :] = own
        col_send[1, at : at + 8, :] = jnp.where(odd_tile, own, roll(inner, -1, 1))
        col_send[0, at : at + 8, :] = jnp.where(odd_tile, roll(inner, 1, 1), own)
    col_copies = cols_copies(col_send, col_recv, 1)
    for copy in col_copies:
        copy.start()

    groups = cols // STRIP
    tiles = rows // 8
    rim_tiles = DEEP // 8
    group_of = lanes((8, cols)) // STRIP

    def strip_of(ref, base, first_row, number):
        strip = None
        for g in range(number):
            at = first_row + 8 * g
            x = roll(ref[at : at + 8, :], STRIP * g - base, 1)
            strip = x if strip is None else jnp.where(group_of == g, x, strip)
        return strip

    def pack_strips(pair, f):
        ref = deep.at[2 * pair + f, 0]
        for side, base in ((0, cols - STRIP), (1, 0)):
            for t in range(0, tiles, groups):
                at = 8 * (t // groups)
                strip_send[pair, side, f, at : at + 8, :] = strip_of(
                    ref, base, start + 8 * t, min(groups, tiles - t)
                )
            for corner, first_row in ((side, stop - DEEP), (2 + side, start)):
                corner_send[pair, corner, 8 * f : 8 * f + 8, :] = strip_of(ref, base, first_row, rim_tiles)

    def fill(pair, f, at, west_tile, east_tile, g):
        low = roll(east_tile, -STRIP * g, 1)
        high = roll(west_tile, cols - STRIP - STRIP * g, 1)
        deep[2 * pair + f, 1, at : at + 8, :] = jnp.where(group_of < groups // 2, low, high)

    def unpack_strips(pair, f, sign):
        for j in range(tiles):
            at = 8 * (j // groups)
            west_tile = strip_recv[pair, 0, f, at : at + 8, :]
            east_tile = strip_recv[pair, 1, f, at : at + 8, :]
            fill(pair, f, start + 8 * j, west_tile, east_tile, j % groups)
        tile_at = slice(8 * f, 8 * f + 8)

        @pl.when(top)
        def _():
            for corner in range(2):
                tile = folded(corner_recv[pair, corner, tile_at, :])
                corner_recv[pair, corner, tile_at, :] = sign * roll(tile, -STRIP, 1)

        for j in range(rim_tiles):
            fill(pair, f, stop + 8 * j, corner_recv[pair, 1, tile_at, :], corner_recv[pair, 0, tile_at, :], j)
            fill(
                pair, f, PAD + 8 * j, corner_recv[pair, 3, tile_at, :], corner_recv[pair, 2, tile_at, :], j
            )

    turned_lon = (lax.rem(2 * n_lon - 2 - lon, n_lon), lax.rem(n_lon - lon, n_lon))
    alone = [jnp.logical_and(top, turned == lon) for turned in turned_lon]

    def corner_copy(pair, corner, slot, device):
        size = 24 if pair == 0 else 16
        return remote(
            corner_send.at[pair, corner, 0:size, :],
            corner_recv.at[pair, slot, 0:size, :],
            corner_send_sems.at[pair, corner],
            corner_recv_sems.at[pair, slot],
            device,
        )

    def corners_out(pair):
        for corner in range(2):
            side = right if corner == 0 else left

            @pl.when(jnp.logical_not(top))
            def _():
                corner_copy(pair, corner, 3 - corner, {"lat": above, "lon": side}).start()

            @pl.when(jnp.logical_and(top, turned_lon[corner] != lon))
            def _():
                corner_copy(pair, corner, corner, {"lon": turned_lon[corner]}).start()

            @pl.when(alone[corner])
            def _():
                corner_recv[pair, corner] = corner_send[pair, corner]

            @pl.when(jnp.logical_not(bottom))
            def _():
                corner_copy(pair, 2 + corner, 1 - corner, {"lat": below, "lon": side}).start()

    def corners_each(pair, act):
        for corner in range(2):
            side = right if corner == 0 else left

            @pl.when(jnp.logical_not(alone[corner]))
            def _():
                act(corner_copy(pair, corner, corner, {"lat": above, "lon": side}))

            @pl.when(jnp.logical_not(bottom))
            def _():
                act(corner_copy(pair, 2 + corner, 2 + corner, {"lat": below, "lon": side}))

    for corner in range(4):
        at = rows - 8 if corner < 2 else 0
        corner_send[0, corner, 16:24, :] = own_pack[PAD + at : PAD + at + 8, :]
    for f in range(2):
        pack_strips(0, f)
    corners_out(0)
    stat_copies = cols_copies(strip_send.at[0], strip_recv.at[0], 2)
    for copy in stat_copies:
        copy.start()

    def edge_of(pair, i):
        at = stop - DEEP if i == 0 else start
        return deep.at[2 * pair : 2 * pair + 2, 0, at : at + DEEP, :]

    stat_edge = lambda i: edge_of(0, i)
    stat_dst = lambda i: fold_recv.at[0, i]
    rows_out(stat_edge, stat_dst, 5)

    def place_rows(pair, sign):
        @pl.when(top)
        def _():
            for f in range(2):
                fold_recv[pair, 0, f] = sign * folded(fold_recv[pair, 0, f])

        for f in range(2):
            deep[2 * pair + f, 0, stop:end, :] = fold_recv[pair, 0, f]

        @pl.when(jnp.logical_not(bottom))
        def _():
            for f in range(2):
                deep[2 * pair + f, 0, PAD:start, :] = fold_recv[pair, 1, f]

    row_ids = (lat * rows + lax.broadcasted_iota(jnp.int32, (rows, cols), 0)).astype(F32)
    coriolis = 0.25 * jnp.sin(math.pi * ((row_ids + 0.5) / (rows * n_lat) - 0.5))
    faces[2, 2, 0:rows, :] = coriolis

    rows_in(row_src, row_dst, 0)

    @pl.when(top)
    def _():
        turned = mirrored(row_recv[0])
        ids = lax.broadcasted_iota(jnp.int32, turned.shape, 0)
        turned = jnp.where(ids < 4 * count, -turned, turned)
        row_recv[0] = turned

    for k in range(kinds):
        ref, index = block_of(k)
        at, both_rows = row_of(k)
        ref[index, top_row : top_row + 1, :] = row_recv[0, at : at + 1, :]
        ref[index, PAD - 1 : PAD, :] = row_recv[1, at : at + 1, :]
        if both_rows:
            ref[index, top_row + 1 : top_row + 2, :] = row_recv[0, at - 1 : at, :]
            ref[index, PAD - 2 : PAD - 1, :] = row_recv[1, at - 1 : at, :]

    for copy in col_copies:
        copy.wait_recv()
    corners_each(0, lambda copy: copy.wait_recv())
    tall = rows + 2 * PAD
    lane = lanes((tall, cols))
    odd = jnp.bitwise_and(lane, 1) == 1
    from_west, from_east = col_recv[0], col_recv[1]
    near[1] = jnp.zeros((tall, cols), F32)
    near[0] = jnp.zeros((tall, cols), F32)
    odd_here = odd[0:rows]
    near[1, PAD:top_row, :] = jnp.where(odd_here, roll(from_west, 1, 1), roll(from_east, -1, 1))
    near[0, PAD:top_row, :] = jnp.where(odd_here, from_west, from_east)
    ne, nw, se, sw = [corner_recv[0, corner, 16:24, :] for corner in range(4)]
    below_tile = jnp.where(odd_tile, roll(sw, 1, 1), roll(se, -1, 1))
    near[1, PAD - 1 : PAD, :] = below_tile[7:8]

    @pl.when(top)
    def _():
        tile = jnp.where(odd_tile, nw, ne)
        tile = jnp.where(lanes((8, cols)) < 4 * count, -tile, tile)
        near[1, top_row : top_row + 1, :] = tile[7:8]

    @pl.when(jnp.logical_not(top))
    def _():
        tile = jnp.where(odd_tile, roll(nw, 1, 1), roll(ne, -1, 1))
        near[1, top_row : top_row + 1, :] = tile[0:1]

    close, far = near[1], near[0]
    own = own_pack[...]

    level_of = lax.rem(jnp.right_shift(lane, 1), count).astype(F32)

    def packed_wet(pack):
        at = 2 * (kinds - 1)
        level = jnp.where(odd, pack[:, at + 1 : at + 2], pack[:, at : at + 1])
        return jnp.where(level_of < level, 1.0, 0.0)

    wet_own, wet_close, wet_far = packed_wet(own), packed_wet(close), packed_wet(far)
    firsts[...] = wet_close * (
        wet_own * (own - close)
        + wet_far * (far - close)
        + roll(wet_close, -1, 0) * (roll(close, -1, 0) - close)
        + roll(wet_close, 1, 0) * (roll(close, 1, 0) - close)
    )

    def sides(x, pack, k):
        rim = pltpu.roll(pack, cols - 1 - 2 * k, 1)
        lane = lanes(x.shape)
        return (
            jnp.where(lane == cols - 1, rim, roll(x, -1, 1)),
            jnp.where(lane == 0, rim, roll(x, 1, 1)),
        )

    whole = slice(PAD, top_row)
    northern = slice(PAD + 1, top_row + 1)
    southern = slice(PAD - 1, top_row - 1)
    for index in range(2):
        c = flats[index, whole, :]
        c_east, c_west = sides(c, near[1, whole, :], 4 * count + index)
        others = (c_east, c_west, flats[index, northern, :], flats[index, southern, :])
        for n, other in enumerate(others):
            faces[index, n, 0:rows, :] = 0.5 * (c + other)
    lev_east, lev_west = sides(flats[2], near[1], kinds - 1)
    faces[2, 0] = lev_east
    faces[2, 1] = lev_west

    def masks(level, here):
        return (
            level < flats[2, here : here + 8, :],
            level < faces[2, 0, here : here + 8, :],
            level < faces[2, 1, here : here + 8, :],
            level < flats[2, here + 1 : here + 9, :],
            level < flats[2, here - 1 : here + 7, :],
        )

    def weighted(x, neighbours, wets, index, at):
        total = None
        for n, other in enumerate(neighbours):
            term = faces[index, n, at : at + 8, :] * jnp.where(wets[n + 1], other - x, 0.0)
            total = term if total is None else total + term
        return total

    def velocity_level(level, carry):
        level_float = level.astype(F32)
        for at in range(0, rows + 8, 8):
            here = PAD - 1 + at
            wets = masks(level_float, here)
            for comp in range(2):
                k = comp * count + level
                x = fields[k, here : here + 8, :]
                x_east, x_west = sides(x, near[1, here : here + 8, :], k)
                first = (
                    jnp.where(wets[1], x_east - x, 0.0)
                    + jnp.where(wets[2], x_west - x, 0.0)
                    + jnp.where(wets[3], fields[k, here + 1 : here + 9, :] - x, 0.0)
                    + jnp.where(wets[4], fields[k, here - 1 : here + 7, :] - x, 0.0)
                )
                laps[comp, at : at + 8, :] = jnp.where(wets[0], first, 0.0)
        for at in range(0, rows, 8):
            here = PAD + at
            wets = masks(level_float, here)
            for comp in range(2):
                k = comp * count + level
                x = laps[comp, at + 1 : at + 9, :]
                x_east, x_west = sides(x, firsts[here : here + 8, :], k)
                others = (x_east, x_west, laps[comp, at + 2 : at + 10, :], laps[comp, at : at + 8, :])
                second = weighted(x, others, wets, 0, at)
                other = fields[(1 - comp) * count + level, here : here + 8, :]
                turned = faces[2, 2, at : at + 8, :] * other
                star = fields[k, here : here + 8, :] - second
                star = jnp.where(wets[0], star + turned if comp == 0 else star - turned, 0.0)
                star_out[k, at : at + 8, :] = star
                deep[2 + comp, 0, start + at : start + at + 8, :] += star
        return carry

    lax.fori_loop(0, count, velocity_level, 0)

    levels_here = flats[2, whole, :]
    ocean_here = jnp.where(levels_here > 0, 1.0, 0.0)
    for comp in range(2):
        mean = deep[2 + comp, 0, start:stop, :] / jnp.maximum(levels_here, 1.0)
        extra_out[comp] = mean
        deep[2 + comp, 0, start:stop, :] = mean + wind[comp] * ocean_here

    flow_edge = lambda i: edge_of(1, i)
    fold_dst = lambda i: fold_recv.at[1, i]
    rows_out(flow_edge, fold_dst, 3)
    for comp in range(2):
        pack_strips(1, comp)
    flow_copies = cols_copies(strip_send.at[1], strip_recv.at[1], 4)
    for copy in flow_copies:
        copy.start()
    corners_out(1)
    stores = [pltpu.make_async_copy(star_out, star_hbm_out, store_sems.at[0])]
    stores[0].start()

    def tracer_level(level, carry):
        for at in range(0, rows, 8):
            here = PAD + at
            wets = masks(level.astype(F32), here)
            for comp in range(2):
                k = 2 * count + comp * count + level
                x = fields[k, here : here + 8, :]
                x_east, x_west = sides(x, near[1, here : here + 8, :], k)
                others = (x_east, x_west, fields[k, here + 1 : here + 9, :], fields[k, here - 1 : here + 7, :])
                change = weighted(x, others, wets, 1, at)
                tracer_out[comp * count + level, at : at + 8, :] = x + jnp.where(wets[0], change, 0.0)
        return carry

    lax.fori_loop(0, count, tracer_level, 0)
    stores.append(pltpu.make_async_copy(tracer_out, tracer_hbm_out, store_sems.at[1]))
    stores[1].start()

    for copy in stat_copies:
        copy.wait_recv()
    rows_in(stat_edge, stat_dst, 5)
    place_rows(0, 1.0)
    for f in range(2):
        unpack_strips(0, f, 1.0)
    both = range(2)

    def around(ref, at):
        result = []
        for shift in (0, 1, -1):
            p = [ref[n, at + shift : at + shift + 8, :] for n in both]
            result += list(lane_sides(*p)) + ([] if shift == 0 else [p])
        return result

    scales = (1.0, 1.0, 0.5, 0.5, 1.0, 0.5, 0.5, 1.0)
    for tile in both:
        ocean[tile, PAD:end, :] = jnp.where(deep[1, tile, PAD:end, :] > 0, 1.0, 0.0)
    for at in range(0, deep_rows, 8):
        depth_here = [deep[0, n, PAD + at : PAD + at + 8, :] for n in both]
        wet_here = [ocean[n, PAD + at : PAD + at + 8, :] for n in both]
        totals = [floor_diag * wet_here[n] + (1.0 - wet_here[n]) for n in both]
        sums = zip(scales, around(deep.at[0], PAD + at), around(ocean, PAD + at))
        for index, (scale, d, o) in enumerate(sums):
            for n in both:
                weight = scale * 0.5 * (depth_here[n] + d[n]) * wet_here[n] * o[n]
                weights[index, n, at : at + 8, :] = weight
                totals[n] = totals[n] + weight
        for n in both:
            weights[8, n, at : at + 8, :] = totals[n]
            weights[9, n, at : at + 8, :] = 0.5 * flow_step * wet_here[n]
            weights[10, n, at : at + 8, :] = 0.5 * slope_step * wet_here[n]

    for copy in flow_copies:
        copy.wait_recv()
    corners_each(1, lambda copy: copy.wait_recv())
    rows_in(flow_edge, fold_dst, 3)
    for comp in range(2):
        unpack_strips(1, comp, -1.0)

    place_rows(1, -1.0)
    rows_sent(flow_edge, fold_dst, 3)

    def subcycle(step, carry):
        for at in range(0, deep_rows, 8):
            here = slice(PAD + at, PAD + at + 8)
            up = slice(PAD + at + 1, PAD + at + 9)
            down = slice(PAD + at - 1, PAD + at + 7)
            easts, wests = lane_sides(*[deep[0, n, here, :] * deep[2, n, here, :] for n in both])
            for n in both:
                divergence = (easts[n] - wests[n]) + (
                    deep[0, n, up, :] * deep[3, n, up, :] - deep[0, n, down, :] * deep[3, n, down, :]
                )
                basis[0, n, here, :] = basis[0, n, here, :] - weights[9, n, at : at + 8, :] * divergence
        for at in range(0, deep_rows, 8):
            here = slice(PAD + at, PAD + at + 8)
            easts, wests = lane_sides(*[basis[0, n, here, :] for n in both])
            for n in both:
                slope = weights[10, n, at : at + 8, :]
                deep[2, n, here, :] = deep[2, n, here, :] - slope * (easts[n] - wests[n])
                deep[3, n, here, :] = deep[3, n, here, :] - slope * (
                    basis[0, n, PAD + at + 1 : PAD + at + 9, :] - basis[0, n, PAD + at - 1 : PAD + at + 7, :]
                )
        return carry

    lax.fori_loop(0, SUBCYCLES, subcycle, 0)

    for k in range(SOLVE_ITERS):
        for at in range(0, deep_rows, 8):
            here = slice(PAD + at, PAD + at + 8)
            summed = [(weights[8, n, at : at + 8, :] - SHIFTS[k]) * basis[k, n, here, :] for n in both]
            for index, term in enumerate(around(basis.at[k], PAD + at)):
                for n in both:
                    summed[n] = summed[n] - weights[index, n, at : at + 8, :] * term[n]
            for n in both:
                basis[k + 1, n, here, :] = summed[n] * (1.0 / SCALE)

    pairs = [(i, j) for i in range(SOLVE_ITERS) for j in range(i, SOLVE_ITERS + 1)]
    products = [None] * len(pairs)
    for at in range(start, stop, 8):
        inside = [basis[k, 0, at : at + 8, :] for k in range(SOLVE_ITERS + 1)]
        for n, (i, j) in enumerate(pairs):
            term = inside[i] * inside[j]
            products[n] = term if products[n] is None else products[n] + term
    lane_row = lanes((1, cols))
    packed_sums = jnp.zeros((1, cols), F32)
    for n, (i, j) in enumerate(pairs):
        value = jnp.sum(jnp.sum(products[n], axis=0, keepdims=True), axis=1, keepdims=True)
        packed_sums = jnp.where(lane_row == n, value, packed_sums)
    me = lat * n_lon + lon
    part[0] = packed_sums

    others = n_lon * n_lat - 1
    for k in range(1, others + 1):
        remote(part, parts.at[pl.ds(me, 1)], sum_send.at[0], sum_recv.at[0], peer(k)).start()
    every = parts.at[0:others]
    remote(every, every, sum_send.at[0], sum_recv.at[0], peer(1)).wait_recv()
    sums = None
    for n in range(others + 1):
        term = jnp.where(me == n, packed_sums, parts[n])
        sums = term if sums is None else sums + term
    sums = jnp.broadcast_to(sums, (8, cols))
    gram = {}
    for n, (i, j) in enumerate(pairs):
        gram[i, j] = gram[j, i] = jnp.broadcast_to(sums[:, n : n + 1], (8, cols))

    def inner_product(a, b):
        result = None
        for i, x in a.items():
            for j, y in b.items():
                term = x * y * gram[i, j]
                result = term if result is None else result + term
        return result

    def image_of(a):
        result = {}
        for n, x in a.items():
            for at, value in ((n, SHIFTS[n] * x), (n + 1, SCALE * x)):
                result[at] = result[at] + value if at in result else value
        return result

    one = jnp.ones((8, cols), F32)
    residual = {0: one}
    direction = {0: one}
    answer = {}
    norm = gram[0, 0]
    for iteration in range(SOLVE_ITERS):
        image = image_of(direction)
        step = norm / inner_product(direction, image)
        for n, x in direction.items():
            answer[n] = answer[n] + step * x if n in answer else step * x
        if iteration < SOLVE_ITERS - 1:
            residual = {n: (residual[n] if n in residual else 0.0) - step * x for n, x in image.items()}
            new_norm = inner_product(residual, residual)
            ratio = new_norm / norm
            direction = {
                n: x + ratio * direction[n] if n in direction else x for n, x in residual.items()
            }
            norm = new_norm
    for at in range(start - 8, stop + 8, 8):
        for tile in both:
            surface = None
            for n, x in answer.items():
                term = x * basis[n, tile, at : at + 8, :]
                surface = term if surface is None else surface + term
            flux[tile, at : at + 8, :] = surface

    easts, wests = lane_sides(flux[0, start:stop, :], flux[1, start:stop, :])
    slopes = (easts[0] - wests[0], flux[0, start + 1 : stop + 1, :] - flux[0, start - 1 : stop - 1, :])
    for comp, slope in enumerate(slopes):
        final = deep[2 + comp, 0, start:stop, :] - weights[10, 0, DEEP : DEEP + rows, :] * slope
        extra_out[comp] = final - extra_out[comp]
    extra_out[2] = levels_here
    extra_out[3] = flux[0, start:stop, :]
    stores.append(pltpu.make_async_copy(extra_out, extra_hbm_out, store_sems.at[2]))
    stores[2].start()
    remote(every, every, sum_send.at[0], sum_recv.at[0], peer(1)).wait_send()
    rows_sent(row_src, row_dst, 0)
    rows_sent(stat_edge, stat_dst, 5)
    for pair in range(2):
        corners_each(pair, lambda copy: copy.wait_send())
    for copy in col_copies + stat_copies + flow_copies:
        copy.wait_send()
    for store in stores:
        store.wait()


def finish(
    tracer_hbm, star_hbm, extra_hbm, tracer_out, velocity_out, surface_out, tracer, star, extra, corrected, sems
):
    count = star.shape[0] // 2
    parts = (slice(0, count), slice(count, 2 * count))
    loads = [
        pltpu.make_async_copy(extra_hbm, extra, sems.at[0]),
        pltpu.make_async_copy(star_hbm.at[parts[0]], star.at[parts[0]], sems.at[1]),
        pltpu.make_async_copy(star_hbm.at[parts[1]], star.at[parts[1]], sems.at[2]),
        pltpu.make_async_copy(tracer_hbm, tracer, sems.at[3]),
    ]
    for load in loads:
        load.start()
    loads[0].wait()
    stores = [pltpu.make_async_copy(extra.at[3], surface_out, sems.at[4])]
    stores[0].start()
    for comp in range(2):
        loads[1 + comp].wait()

        def correct(level, carry):
            k = comp * count + level
            wet = level.astype(F32) < extra[2]
            corrected[k] = star[k] + jnp.where(wet, extra[comp], 0.0)
            return carry

        lax.fori_loop(0, count, correct, 0)
        store = pltpu.make_async_copy(corrected.at[parts[comp]], velocity_out.at[parts[comp]], sems.at[5 + comp])
        store.start()
        stores.append(store)
    loads[3].wait()
    stores.append(pltpu.make_async_copy(tracer, tracer_out, sems.at[7]))
    stores[-1].start()
    for store in stores:
        store.wait()


def per_device(n_lon, n_lat, tracers, velocity, active_levels, diffusivity, viscosity, ocean_depth, wind_forcing):
    _, count, rows, cols = tracers.shape
    message = -(-(6 * count + 4) // 8) * 8
    tall, deep_rows = rows + 2 * PAD, rows + 2 * DEEP
    padded = deep_rows + 2 * PAD
    strip_rows = 8 * -(-(rows // 8) // (cols // STRIP))
    extra = jax.ShapeDtypeStruct((4, rows, cols), F32)
    block = jax.ShapeDtypeStruct((2 * count, rows, cols), F32)
    flat = jax.ShapeDtypeStruct((rows, cols), F32)
    hbm = pl.BlockSpec(memory_space=pltpu.HBM)
    out = pl.pallas_call(
        functools.partial(kernel, n_lon, n_lat),
        out_shape=(block, block, extra),
        in_specs=[hbm] * 7,
        out_specs=(hbm, hbm, hbm),
        scratch_shapes=[
            pltpu.VMEM(block.shape, F32),
            pltpu.VMEM(block.shape, F32),
            pltpu.VMEM(extra.shape, F32),
            pltpu.VMEM((4 * count, tall, cols), F32),
            pltpu.VMEM((3, tall, cols), F32),
            pltpu.VMEM((rows, cols), jnp.int32),
            pltpu.VMEM((2, rows, cols), F32),
            pltpu.VMEM((2, tall, cols), F32),
            pltpu.VMEM((tall, cols), F32),
            pltpu.VMEM((tall, cols), F32),
            pltpu.VMEM((2, tall, cols), F32),
            pltpu.VMEM((3, 4, tall, cols), F32),
            pltpu.VMEM((4, 2, padded, cols), F32),
            pltpu.VMEM((2, padded, cols), F32),
            pltpu.VMEM((11, 2, deep_rows, cols), F32),
            pltpu.VMEM((2, padded, cols), F32),
            pltpu.VMEM((SOLVE_ITERS + 1, 2, padded, cols), F32),
            pltpu.VMEM((2, message, cols), F32),
            pltpu.VMEM((2, message, cols), F32),
            pltpu.VMEM((2, rows, cols), F32),
            pltpu.VMEM((2, rows, cols), F32),
            pltpu.VMEM((2, 2, 2, strip_rows, cols), F32),
            pltpu.VMEM((2, 2, 2, strip_rows, cols), F32),
            pltpu.VMEM((2, 4, 24, cols), F32),
            pltpu.VMEM((2, 4, 24, cols), F32),
            pltpu.VMEM((2, 2, 2, DEEP, cols), F32),
            pltpu.VMEM((1, 1, cols), F32),
            pltpu.VMEM((n_lon * n_lat, 1, cols), F32),
            pltpu.SemaphoreType.DMA((7,)),
            pltpu.SemaphoreType.DMA((3,)),
            pltpu.SemaphoreType.DMA((6, 2)),
            pltpu.SemaphoreType.DMA((6, 2)),
            pltpu.SemaphoreType.DMA((2, 4)),
            pltpu.SemaphoreType.DMA((2, 4)),
            pltpu.SemaphoreType.DMA((1,)),
            pltpu.SemaphoreType.DMA((1,)),
        ],
        compiler_params=pltpu.CompilerParams(
            collective_id=0, has_side_effects=True, vmem_limit_bytes=58 * 1024 * 1024
        ),
    )(
        tracers.reshape(2 * count, rows, cols),
        velocity.reshape(2 * count, rows, cols),
        active_levels,
        diffusivity,
        viscosity,
        ocean_depth,
        wind_forcing,
    )
    out = pl.pallas_call(
        finish,
        out_shape=(block, block, flat),
        in_specs=[hbm] * 3,
        out_specs=(hbm, hbm, hbm),
        scratch_shapes=[
            pltpu.VMEM(block.shape, F32),
            pltpu.VMEM(block.shape, F32),
            pltpu.VMEM(extra.shape, F32),
            pltpu.VMEM(block.shape, F32),
            pltpu.SemaphoreType.DMA((8,)),
        ],
        compiler_params=pltpu.CompilerParams(vmem_limit_bytes=58 * 1024 * 1024),
    )(*out)
    return out[0].reshape(tracers.shape), out[1].reshape(velocity.shape), out[2]


def solution(mesh):
    flat = P("lat", "lon")
    deep = P(None, None, "lat", "lon")
    return jax.shard_map(
        functools.partial(per_device, mesh.shape["lon"], mesh.shape["lat"]),
        mesh=mesh,
        in_specs=(deep, deep, flat, flat, flat, flat, P(None, "lat", "lon")),
        out_specs=(deep, deep, flat),
        check_vma=False,
    )
```
